256 devices in a mesh: pair: 8 (over y_lo, x), grow: 8 (over z), gcol: 4 (over y_hi, core).
Axes of the slice: x: 4, y: 4 (y_hi: 2, y_lo: 2; y = y_hi * 2 + y_lo), z: 8, core: 2. Of those that a mesh axis runs over, the one named last changes fastest.
Arguments:
- valence: bfloat16 [2, 64, 128, 16384], P(None, None, ('grow', 'gcol')), may hold values from -6 to 6
- conduction: bfloat16 [2, 8, 128, 16384], P(None, 'pair', ('grow', 'gcol')), may hold values from -6 to 6
- pair_bands: int32 [8, 32], P('pair'), may hold values from 0 to 63, as said below
- e_val: float32 [64], replicated, may hold values from -12 to -1
- e_cond: float32 [8], P('pair'), may hold values from 1 to 12
- g_index: int32 [30720], replicated, may hold values from 0 to 2097151, as said below
- slab_index: int32 [2048], replicated, may hold values from 0 to 2097151, as said below
Outputs:
- chi_slab: float32 [2, 30720, 2048], P(None, ('pair', 'grow'), 'gcol')
The draws below stay inside these ranges and needn't reach their ends.
Inputs may be any that keep to these rules, and one draw needn't show every extreme that they name: `pair_bands`: each row lists 32 different valence bands. All entries of g_index and slab_index name different grid points. Write G = ((p * 8 + g) * 4 + c) * 120 + j with j < 120; the grid point of row G has q2 within [c * 32, (c + 1) * 32) and q3 within [b w, (b + 1) w) with b = g * 4 + c and w = 4. `slab_index`: write H = ((c * 8 + p) * 8 + g) * 8 + j with j < 8; the grid point of column H lies in the same range of q2 and q3 as the rows of g_index with these g and c.
All inputs are finite; a program needn't handle non-finite values.
Results may differ from the reference program's by a relative error of at most 0.012.
Values may be sent and summed in bfloat16 or wider, within the bound.
No kernel may reach another device: no remote copies, remote signals or barrier semaphores. Data moves between devices by JAX's collectives and lax.ppermute only.
A program may use at most 192 MiB of HBM per device.

```python
import math
import jax
import jax.numpy as jnp
from jax import lax

NGRID = 128
NVAL = 64
PV = 32
GQ = 120
GCQ = 8
NC = 8
PAIRS = 256
NG = 30720
GC = 2048
N_PAIR = 8
N_GROW = 8
N_GCOL = 4


def grid_picks(key):
    blocks = N_GROW * N_GCOL
    planes = NGRID // blocks
    wide_two = NGRID // N_GCOL
    count = NGRID * wide_two * planes
    keys = jax.random.split(key, blocks)
    orders = jax.vmap(lambda one: jax.random.permutation(one, count))(keys)
    needed = N_PAIR * (GQ + GCQ)
    offsets = orders[:, :needed].astype(jnp.int32)
    block_ids = jnp.arange(blocks, dtype=jnp.int32)
    gcol_of = block_ids % N_GCOL
    first = offsets // (wide_two * planes)
    second = gcol_of[:, None] * wide_two + offsets // planes % wide_two
    third = block_ids[:, None] * planes + offsets % planes
    return ((first * NGRID + second) * NGRID + third).astype(jnp.int32)


def draw_g_index(key, part):
    picks = grid_picks(key)
    rows = picks[:, :N_PAIR * GQ].reshape(N_GROW, N_GCOL, N_PAIR, GQ)
    return jnp.transpose(rows, (2, 0, 1, 3)).reshape(-1).astype(jnp.int32)


def draw_slab_index(key, part):
    picks = grid_picks(key)
    cols = picks[:, N_PAIR * GQ:].reshape(N_GROW, N_GCOL, N_PAIR, GCQ)
    return jnp.transpose(cols, (1, 2, 0, 3)).reshape(-1).astype(jnp.int32)


def draw_pair_bands(key, part):
    key = jax.random.fold_in(key, 3)
    keys = jax.random.split(key, NC + 2)
    chosen = jax.vmap(lambda one: jax.random.permutation(one, NVAL)[:PV])(keys[:NC])
    middle = jax.random.permutation(keys[NC], NVAL - 2)[:PV - 2] + 1
    ends = jnp.array([0, NVAL - 1], dtype=jnp.int32)
    first_row = jax.random.permutation(keys[NC + 1], jnp.concatenate([ends, middle.astype(jnp.int32)]))
    chosen = chosen.astype(jnp.int32).at[0].set(first_row.astype(jnp.int32))
    return chosen.astype(jnp.int32)


def levels(stream_key, shape, shards, low, top_value):
    gain, own = 1.0, jax.random.fold_in(stream_key, 6)
    for position, parts in shards:
        draws = jnp.exp(jax.random.uniform(jax.random.fold_in(own, position), (parts,), jnp.float32, low / len(shards), top_value / len(shards)))
        gain = gain * jnp.repeat(draws, shape[position] // parts).reshape([-1 if axis == position else 1 for axis in range(len(shape))])
    return gain


def scatter_about(key, shape, width, bound, shards=(), kind=jnp.bfloat16):
    gain = levels(key, shape, shards, -0.22, 0.18) if shards else 1.0
    drawn = jax.random.normal(key, shape, jnp.float32) * width * gain
    return jnp.minimum(jnp.maximum(drawn, -bound), bound).astype(kind)


def setup_inputs(seed: int = 0) -> dict:
    key_list = jax.random.split(jax.random.key(seed), 8)
    return {
        "valence": scatter_about(key_list[0], (2, NVAL, NGRID, NGRID * NGRID), 1.0, 6.0, ((2, 32),)),
        "conduction": scatter_about(key_list[1], (2, NC, NGRID, NGRID * NGRID), 1.0, 6.0, ((1, 8), (2, 32))),
        "pair_bands": draw_pair_bands(jax.random.fold_in(key_list[7], 71), 0),
        "e_val": jnp.clip(jax.random.uniform(key_list[3], (NVAL,), jnp.float32, -12.0, -1.0), -12.0, -1.0),
        "e_cond": jnp.clip(1.0 + 11.0 * jax.random.uniform(key_list[4], (NC,), jnp.float32) ** levels(key_list[4], (NC,), ((0, 8),), -0.2, 0.2), 1.0, 12.0),
        "g_index": draw_g_index(jax.random.fold_in(key_list[7], 71), 0),
        "slab_index": draw_slab_index(jax.random.fold_in(key_list[7], 71), 0),
    }


def transform_table(count):
    freq = jnp.arange(count, dtype=jnp.int32)
    phase = freq[:, None] * freq[None, :] % count
    angle = phase.astype(jnp.float32) * (2.0 * math.pi / count)
    scale = 1.0 / math.sqrt(count)
    cosine = (jnp.cos(angle) * scale).astype(jnp.bfloat16)
    sine = (jnp.sin(angle) * scale).astype(jnp.bfloat16)
    upper = jnp.stack([cosine, sine], axis=1)
    lower = jnp.stack([-sine, cosine], axis=1)
    return jnp.stack([upper, lower]).astype(jnp.float32)

def reference(valence, conduction, pair_bands, e_val, e_cond, g_index, slab_index):
    table = transform_table(NGRID)
    val_grid = valence.reshape(2, NVAL, NGRID, NGRID, NGRID)
    cond_grid = conduction.reshape(2, NC, NGRID, NGRID, NGRID)

    def one_band(band):
        chosen = pair_bands[band]
        picked = jnp.take(val_grid, chosen, axis=1).astype(jnp.float32)
        cond_now = cond_grid[:, band].astype(jnp.float32)
        real_part = picked[0] * cond_now[0][None] + picked[1] * cond_now[1][None]
        imag_part = picked[0] * cond_now[1][None] - picked[1] * cond_now[0][None]
        density = jnp.stack([real_part, imag_part]).astype(jnp.bfloat16)
        density = jnp.moveaxis(density, 1, 4).astype(jnp.float32)
        third = jnp.einsum('okix,iabxp->oabkp', table, density).astype(jnp.bfloat16)
        second = jnp.einsum('okix,iaxbp->oakbp', table, third.astype(jnp.float32)).astype(jnp.bfloat16)
        first = jnp.einsum('okix,ixabp->okabp', table, second.astype(jnp.float32)).astype(jnp.bfloat16)
        flat = first.reshape(2, NGRID * NGRID * NGRID, PV)
        weight = 2.0 / ((jnp.take(e_val, chosen) - e_cond[band]) * math.sqrt(PAIRS))
        rows = (jnp.take(flat, g_index, axis=1).astype(jnp.float32) * weight).astype(jnp.bfloat16)
        cols = jnp.take(flat, slab_index, axis=1)
        return (rows, cols)
    rows, cols = lax.map(one_band, jnp.arange(NC, dtype=jnp.int32))
    rows = jnp.transpose(rows, (1, 2, 0, 3)).reshape(2, NG, PAIRS).astype(jnp.float32)
    cols = jnp.transpose(cols, (1, 2, 0, 3)).reshape(2, GC, PAIRS).astype(jnp.float32)
    real_out = jnp.dot(rows[0], cols[0].T, preferred_element_type=jnp.float32) + jnp.dot(rows[1], cols[1].T, preferred_element_type=jnp.float32)
    imag_out = jnp.dot(rows[1], cols[0].T, preferred_element_type=jnp.float32) - jnp.dot(rows[0], cols[1].T, preferred_element_type=jnp.float32)
    return jnp.stack([real_out, imag_out])
```

```python
import math
import numpy as np
import ml_dtypes
import jax
import jax.numpy as jnp
from jax import lax
from jax.sharding import PartitionSpec as P
from jax.experimental import pallas as pl
from jax.experimental.pallas import tpu as pltpu
BF=jnp.bfloat16
NG=128; GR=8; GC=4; PL=4; QW=32; PAIRS=32; J=4
NT=(((1,),(1,)),((),()))
NN=(((1,),(0,)),((),()))

def cs(freq,pos):
    ph=(freq[:,None]*pos[None,:])%NG
    ang=ph.astype(np.float64)*(2*math.pi/NG)
    return np.cos(ang)/math.sqrt(NG), np.sin(ang)/math.sqrt(NG)

def tables():
    ar=np.arange(NG)
    c,w,g=np.meshgrid(np.arange(GC),np.arange(PL),np.arange(GR),indexing="ij")
    q3=((g*GC+c)*PL+w).reshape(-1)
    co,si=cs(q3,ar)
    t3=np.block([[co,si],[-si,co]])
    t2=np.zeros((GC,J,2,NG,2,J,QW))
    for cc in range(GC):
        co,si=cs(cc*QW+np.arange(QW),ar)
        for j in range(J):
            t2[cc,j,0,:,0,j,:]=co.T
            t2[cc,j,1,:,0,j,:]=si.T
            t2[cc,j,0,:,1,j,:]=-si.T
            t2[cc,j,1,:,1,j,:]=co.T
    t2=t2.reshape(GC,J*2*NG,2*J*QW)
    perm=np.zeros((256,256))
    for cc in range(GC):
        for s in range(PL):
            for o in range(2):
                for g_ in range(GR):
                    perm[((g_*GC+cc)*PL+s)*2+o, ((cc*PL+s)*2+o)*GR+g_]=1
    return [np.asarray(t,np.float32).astype(ml_dtypes.bfloat16) for t in (t3,t2,perm)]

def kern_a(bands, v0,v1,v2,v3, cond, t3, t2, perm, out, vs, third):
    for j,v in enumerate((v0,v1,v2,v3)):
        vs[0]=v[0,0].astype(jnp.float32)
        vs[1]=v[1,0].astype(jnp.float32)
        for sp in range(PL//2):
            rows=[]
            for s in (2*sp,2*sp+1):
                vr=vs[0,pl.ds(s,NG,stride=PL),:]
                vi=vs[1,pl.ds(s,NG,stride=PL),:]
                cr=cond[0,s]
                ci=cond[1,s]
                re=vr*cr+vi*ci
                im=vr*ci-vi*cr
                rows.append(jnp.concatenate([re.astype(BF),im.astype(BF)],axis=1))
            d=jnp.concatenate(rows,axis=0)
            th=lax.dot_general(t3[...],d,NT,preferred_element_type=jnp.float32)
            third[j,sp]=th.astype(BF)
    ys=[]
    for c in range(GC):
        lhs=[]
        for s in range(PL):
            lhs.append(jnp.concatenate([third[j,s//2,i*NG+c*QW:i*NG+(c+1)*QW,(s%2)*NG:(s%2+1)*NG] for j in range(J) for i in range(2)],axis=1))
        lhs=jnp.concatenate(lhs,axis=0)
        ys.append(jnp.dot(lhs,t2[c],preferred_element_type=jnp.float32))
    for wp in range(PL//2):
        cols=[]
        for w in (2*wp,2*wp+1):
            pieces=[ys[c][s*QW+w*GR:s*QW+(w+1)*GR,o*NG:(o+1)*NG] for c in range(GC) for s in range(PL) for o in range(2)]
            cols.append(jnp.concatenate(pieces,axis=0).astype(BF))
        y=jnp.concatenate(cols,axis=1)
        out[:,wp*256:(wp+1)*256]=jnp.dot(perm[...],y,preferred_element_type=jnp.float32).astype(BF)

def stage_a(valence, cond, bands):
    nval=valence.shape[1]
    v=jnp.transpose(valence.reshape(2,nval,PL,NG,NG),(0,1,3,2,4)).reshape(2,nval,NG*PL,NG)
    cf=cond.reshape(2,PL,NG,NG).astype(jnp.float32)
    t3,t2,perm=tables()
    def vspec(j):
        return pl.BlockSpec((2,1,NG*PL,NG),lambda q,b: (0,b[q*J+j],0,0))
    full=lambda shape: pl.BlockSpec(shape,lambda q,b:(0,)*len(shape))
    return pl.pallas_call(kern_a,
        grid_spec=pltpu.PrefetchScalarGridSpec(num_scalar_prefetch=1,grid=(bands.shape[0]//J,),
            in_specs=[vspec(j) for j in range(J)]+[full((2,PL,NG,NG)),full((256,256)),full((GC,1024,256)),full((256,256))],
            out_specs=pl.BlockSpec((256,512),lambda q,b:(0,q)),
            scratch_shapes=[pltpu.VMEM((2,NG*PL,NG),jnp.float32),pltpu.VMEM((J,PL//2,256,256),BF)]),
        out_shape=jax.ShapeDtypeStruct((256,bands.shape[0]//J*512),BF),
        compiler_params=pltpu.CompilerParams(vmem_limit_bytes=48*2**20),
        name="partial_transform")(bands,v,v,v,v,cf,t3,t2,perm)

ROWS=GR*64; COLS=32; PTS=ROWS+COLS

def tables_c():
    ar=np.arange(NG)
    co,si=cs(ar,ar)
    t1=np.zeros((NG,2,NG,2))
    t1[:,0,:,0]=co; t1[:,0,:,1]=si; t1[:,1,:,0]=-si; t1[:,1,:,1]=co
    t1=t1.reshape(256,256)
    lp=np.zeros((PAIRS,QW,QW,PAIRS))
    for p in range(PAIRS):
        for q in range(QW):
            lp[p,q,q,p]=1
    lp=lp.reshape(1024,1024)
    pick=np.zeros((2,2,4,PAIRS,2,2,PAIRS))
    for h in range(2):
        for o in range(2):
            for p in range(PAIRS):
                pick[h,o,:,p,h,o,p]=1
    pick=pick.reshape(512,128)
    return [np.asarray(t,np.float32).astype(ml_dtypes.bfloat16) for t in (t1,lp,pick)]

def kern_c(place, x, t1, lp, pick, mask, weight, rows_out, cols_out, field, found):
    for w in range(PL):
        xw=jnp.concatenate([x[:,(q*PL+w)*NG:(q*PL+w+1)*NG] for q in range(8)],axis=1)
        e=jnp.dot(t1[...],xw,preferred_element_type=jnp.float32).astype(BF)
        f=jnp.dot(e,lp[...],preferred_element_type=jnp.float32)
        for t in range(8):
            field[(w*8+t)*256:(w*8+t+1)*256,:]=f[:,t*NG:(t+1)*NG]
    def body(r,carry):
        for h in range(2):
            at=pl.multiple_of(place[2*r+h],2)
            found[pl.ds(pl.multiple_of(4*r+2*h,2),2),:]=field[pl.ds(at,2),:]
        return carry
    lax.fori_loop(0,PTS,body,0,unroll=8)
    parts=[]
    for h in range(2):
        for o in range(2):
            parts.append(found[pl.ds(2*h+o,PTS,stride=4),:].astype(BF)*mask[:,h*NG:(h+1)*NG])
    got=jnp.dot(jnp.concatenate(parts,axis=1),pick[...],preferred_element_type=jnp.float32)
    rows_out[...]=(got[:ROWS]*weight[...]).astype(BF)
    cols_out[...]=got[ROWS:].astype(BF)

def point_lists(g_index, slab_index, n_pair,n_grow,n_gcol,grow_at,gcol_at):
    rc=g_index.shape[0]//(n_pair*n_grow*n_gcol)
    cc=slab_index.shape[0]//(n_pair*n_grow*n_gcol)
    row_ids=g_index.reshape(n_pair,n_grow,n_gcol,rc)[:,grow_at,gcol_at]
    row_ids=jnp.pad(row_ids,((0,0),(0,NG-rc)),mode="edge")
    row_ids=jnp.transpose(row_ids.reshape(n_pair,2,64),(0,2,1)).reshape(ROWS,2)
    col_ids=slab_index.reshape(n_gcol,n_pair,n_grow,cc)[gcol_at,:,grow_at]
    col_ids=jnp.transpose(col_ids.reshape(2,COLS),(1,0))
    return jnp.concatenate([row_ids,col_ids],axis=0)

def stage_c(moved, ids, weight):
    q1=ids//(NG*NG); q2=ids//NG%QW; w=ids%PL
    place=((w*8+q2//4)*256+2*q1).reshape(-1)
    lane=jnp.arange(NG,dtype=jnp.int32)//PAIRS
    mask=((q2%4)[:,:,None]==lane).astype(BF).reshape(PTS,2*NG)
    wl=jnp.tile(weight,4).reshape(1,NG)
    t1,lp,pick=tables_c()
    vm=pl.BlockSpec(memory_space=pltpu.VMEM)
    return pl.pallas_call(kern_c,
        in_specs=[pl.BlockSpec(memory_space=pltpu.SMEM)]+[vm]*6,
        out_specs=[vm,vm],
        out_shape=[jax.ShapeDtypeStruct((ROWS,NG),BF),jax.ShapeDtypeStruct((COLS,NG),BF)],
        scratch_shapes=[pltpu.VMEM((PL*8*256,NG),jnp.float32),pltpu.VMEM((4*PTS,NG),jnp.float32)],
        compiler_params=pltpu.CompilerParams(vmem_limit_bytes=48*2**20),
        name="last_transform")(place,moved,t1,lp,pick,mask,wl)

def tables_d():
    q=np.zeros((2,2,2,PAIRS,2,2,2,2,PAIRS))
    for hc in range(2):
        for hr in range(2):
            for p in range(PAIRS):
                q[hc,hc,0,p,hr,0,hr,0,p]=1
                q[hc,hc,1,p,hr,0,hr,1,p]=1
                q[hc,hc,1,p,hr,1,hr,0,p]=-1
                q[hc,hc,0,p,hr,1,hr,1,p]=1
    q=q.reshape(2,128,512)
    return np.asarray(q,np.float32).astype(ml_dtypes.bfloat16)

def kern_d(rows, cols, turn, out, rhs):
    for p in range(8):
        s=cols[p]
        for hc in range(2):
            v=jnp.dot(s,turn[hc],preferred_element_type=jnp.float32)
            for pb in range(4):
                piece=jnp.concatenate([v[(g*4+pb)*8:(g*4+pb+1)*8] for g in range(8)],axis=0).astype(BF)
                for k in range(4):
                    rhs[k,(hc*4+pb)*64:(hc*4+pb+1)*64,p*NG:(p+1)*NG]=piece[:,k*NG:(k+1)*NG]
    lhs=jnp.concatenate([rows[p] for p in range(8)],axis=1)
    for hr in range(2):
        n=64 if hr==0 else 56
        for o in range(2):
            z=lax.dot_general(lhs,rhs[hr*2+o],NT,preferred_element_type=jnp.float32)
            for c in range(4):
                out[o,c*120+64*hr:c*120+64*hr+n,:]=z[c*64:c*64+n]

def stage_d(rows, cols):
    vm=pl.BlockSpec(memory_space=pltpu.VMEM)
    return pl.pallas_call(kern_d,
        in_specs=[vm]*3,out_specs=vm,
        out_shape=jax.ShapeDtypeStruct((2,480,512),jnp.float32),
        scratch_shapes=[pltpu.VMEM((4,512,1024),BF)],
        compiler_params=pltpu.CompilerParams(vmem_limit_bytes=48*2**20),
        name="pair_sums")(rows,cols,tables_d())

def on_device(valence, conduction, pair_bands, e_val, e_cond, g_index, slab_index):
    n_pair = lax.axis_size("pair")
    n_grow = lax.axis_size("grow")
    n_gcol = lax.axis_size("gcol")
    grow_at = lax.axis_index("grow")
    gcol_at = lax.axis_index("gcol")
    bands = pair_bands.reshape(-1)
    part = stage_a(valence, conduction, bands)
    moved = lax.all_to_all(part.reshape(32, 8, 4096), ("grow", "gcol"), 0, 0, tiled=True)
    ids = point_lists(g_index, slab_index, n_pair, n_grow, n_gcol, grow_at, gcol_at)
    gaps = jnp.take(e_val, bands) - e_cond[0]
    weight = 2.0 / (gaps * math.sqrt(PAIRS * n_pair))
    rows, cols = stage_c(moved.reshape(256, 4096), ids, weight)
    rows = jnp.broadcast_to(rows.reshape(8, 1, 64, NG), (8, 4, 64, NG)).reshape(32, 64, NG)
    rows = lax.all_to_all(rows, ("pair", "gcol"), 0, 0, tiled=True).reshape(8, 256, NG)
    cols = jnp.broadcast_to(cols[None], (64, COLS, NG))
    cols = lax.all_to_all(cols, ("pair", "grow"), 0, 0, tiled=True).reshape(8, 256, NG)
    return stage_d(rows, cols)


def solution(mesh):
    in_specs = (
        P(None, None, ("grow", "gcol"), None),
        P(None, "pair", ("grow", "gcol"), None),
        P("pair", None),
        P(),
        P("pair"),
        P(),
        P(),
    )
    out_specs = P(None, ("pair", "grow"), "gcol")
    return jax.shard_map(
        on_device, mesh=mesh, in_specs=in_specs, out_specs=out_specs, check_vma=False
    )
```

```python
import math
import numpy as np
import ml_dtypes
import jax
import jax.numpy as jnp
from jax import lax
from jax.sharding import PartitionSpec as P
from jax.experimental import pallas as pl
from jax.experimental.pallas import tpu as pltpu
BF=jnp.bfloat16
NG=128; GR=8; GC=4; PL=4; QW=32; PAIRS=32; J=4
NT=(((1,),(1,)),((),()))
NN=(((1,),(0,)),((),()))

def cs(freq,pos):
    ph=(freq[:,None]*pos[None,:])%NG
    ang=ph.astype(np.float64)*(2*math.pi/NG)
    return np.cos(ang)/math.sqrt(NG), np.sin(ang)/math.sqrt(NG)

def tables():
    ar=np.arange(NG)
    c,w,g=np.meshgrid(np.arange(GC),np.arange(PL),np.arange(GR),indexing="ij")
    q3=((g*GC+c)*PL+w).reshape(-1)
    co,si=cs(q3,ar)
    t3=np.block([[co,si],[-si,co]])
    t2=np.zeros((GC,J,2,NG,2,J,QW))
    for cc in range(GC):
        co,si=cs(cc*QW+np.arange(QW),ar)
        for j in range(J):
            t2[cc,j,0,:,0,j,:]=co.T
            t2[cc,j,1,:,0,j,:]=si.T
            t2[cc,j,0,:,1,j,:]=-si.T
            t2[cc,j,1,:,1,j,:]=co.T
    t2=t2.reshape(GC,J*2*NG,2*J*QW)
    perm=np.zeros((256,256))
    for cc in range(GC):
        for s in range(PL):
            for o in range(2):
                for g_ in range(GR):
                    perm[((g_*GC+cc)*PL+s)*2+o, ((cc*PL+s)*2+o)*GR+g_]=1
    return [np.asarray(t,np.float32).astype(ml_dtypes.bfloat16) for t in (t3,t2,perm)]

def kern_a(bands, v0, v1, v2, v3, cnd, t3_hbm, t2_hbm, perm_hbm, out, vs, third, cond, t3, t2, perm, sems):
    first = pl.program_id(0) == 0
    loads = [pltpu.make_async_copy(a, b, sems.at[k]) for k, (a, b) in enumerate(((t3_hbm, t3), (t2_hbm, t2), (perm_hbm, perm)))]

    @pl.when(first)
    def _():
        for load in loads:
            load.start()
        for i in range(2):
            vs[i] = cnd[i].astype(jnp.float32)
            for s in range(PL):
                cond[i, s] = vs[i, pl.ds(s, NG, stride=PL), :]
        loads[0].wait()

    for j,v in enumerate((v0,v1,v2,v3)):
        vs[0]=v[0,0].astype(jnp.float32)
        vs[1]=v[1,0].astype(jnp.float32)
        for sp in range(PL//2):
            rows=[]
            for s in (2*sp,2*sp+1):
                vr=vs[0,pl.ds(s,NG,stride=PL),:]
                vi=vs[1,pl.ds(s,NG,stride=PL),:]
                cr=cond[0,s]
                ci=cond[1,s]
                re=vr*cr+vi*ci
                im=vr*ci-vi*cr
                rows.append(jnp.concatenate([re.astype(BF),im.astype(BF)],axis=1))
            d=jnp.concatenate(rows,axis=0)
            th=lax.dot_general(t3[...],d,NT,preferred_element_type=jnp.float32)
            third[j,sp]=th.astype(BF)
    @pl.when(first)
    def _():
        loads[1].wait()
        loads[2].wait()

    ys=[]
    for c in range(GC):
        lhs=[]
        for s in range(PL):
            lhs.append(jnp.concatenate([third[j,s//2,i*NG+c*QW:i*NG+(c+1)*QW,(s%2)*NG:(s%2+1)*NG] for j in range(J) for i in range(2)],axis=1))
        lhs=jnp.concatenate(lhs,axis=0)
        ys.append(jnp.dot(lhs,t2[c],preferred_element_type=jnp.float32))
    for wp in range(PL//2):
        cols=[]
        for w in (2*wp,2*wp+1):
            pieces=[ys[c][s*QW+w*GR:s*QW+(w+1)*GR,o*NG:(o+1)*NG] for c in range(GC) for s in range(PL) for o in range(2)]
            cols.append(jnp.concatenate(pieces,axis=0).astype(BF))
        y=jnp.concatenate(cols,axis=1)
        out[:,wp*256:(wp+1)*256]=jnp.dot(perm[...],y,preferred_element_type=jnp.float32).astype(BF)

def stage_a(valence, cond, bands):
    nval=valence.shape[1]
    v=jnp.transpose(valence.reshape(2,nval,PL,NG,NG),(0,1,3,2,4)).reshape(2,nval,NG*PL,NG)
    cf=jnp.transpose(cond.reshape(2,PL,NG,NG),(0,2,1,3)).reshape(2,NG*PL,NG)
    t3,t2,perm=tables()
    def vspec(j):
        return pl.BlockSpec((2,1,NG*PL,NG),lambda q,b: (0,b[q*J+j],0,0))
    full=lambda shape: pl.BlockSpec(shape,lambda q,b:(0,)*len(shape))
    return pl.pallas_call(kern_a,
        grid_spec=pltpu.PrefetchScalarGridSpec(num_scalar_prefetch=1,grid=(bands.shape[0]//J,),
            in_specs=[vspec(j) for j in range(J)]+[full((2,NG*PL,NG))]+[pl.BlockSpec(memory_space=pltpu.HBM)]*3,
            out_specs=pl.BlockSpec((256,512),lambda q,b:(0,q)),
            scratch_shapes=[pltpu.VMEM((2,NG*PL,NG),jnp.float32),pltpu.VMEM((J,PL//2,256,256),BF),pltpu.VMEM((2,PL,NG,NG),jnp.float32),pltpu.VMEM((256,256),BF),pltpu.VMEM((GC,1024,256),BF),pltpu.VMEM((256,256),BF),pltpu.SemaphoreType.DMA((3,))]),
        out_shape=jax.ShapeDtypeStruct((256,bands.shape[0]//J*512),BF),
        compiler_params=pltpu.CompilerParams(vmem_limit_bytes=48*2**20),
        name="partial_transform")(bands,v,v,v,v,cf,t3,t2,perm)

ROWS=GR*64; COLS=32; PTS=ROWS+COLS

def tables_c():
    ar=np.arange(NG)
    co,si=cs(ar,ar)
    t1=np.zeros((NG,2,NG,2))
    t1[:,0,:,0]=co; t1[:,0,:,1]=si; t1[:,1,:,0]=-si; t1[:,1,:,1]=co
    t1=t1.reshape(256,256)
    lp=np.zeros((PAIRS,QW,QW,PAIRS))
    for p in range(PAIRS):
        for q in range(QW):
            lp[p,q,q,p]=1
    lp=lp.reshape(1024,1024)
    pick=np.zeros((2,2,4,PAIRS,2,2,PAIRS))
    for h in range(2):
        for o in range(2):
            for p in range(PAIRS):
                pick[h,o,:,p,h,o,p]=1
    pick=pick.reshape(512,128)
    return [np.asarray(t,np.float32).astype(ml_dtypes.bfloat16) for t in (t1,lp,pick)]

def kern_c(place, x, t1, lp_hbm, pick, mask, weight, rows_out, cols_out, field, found, lp, sem):
    load = pltpu.make_async_copy(lp_hbm, lp, sem)
    load.start()
    for w in range(PL):
        xw=jnp.concatenate([x[:,(q*PL+w)*NG:(q*PL+w+1)*NG] for q in range(8)],axis=1)
        e=jnp.dot(t1[...],xw,preferred_element_type=jnp.float32).astype(BF)
        if w==0:
            load.wait()
        f=jnp.dot(e,lp[...],preferred_element_type=jnp.float32)
        for t in range(8):
            field[(w*8+t)*256:(w*8+t+1)*256,:]=f[:,t*NG:(t+1)*NG]
    def body(r,carry):
        for h in range(2):
            at=pl.multiple_of(place[2*r+h],2)
            found[pl.ds(pl.multiple_of(4*r+2*h,2),2),:]=field[pl.ds(at,2),:]
        return carry
    lax.fori_loop(0,PTS,body,0,unroll=8)
    parts=[]
    for h in range(2):
        for o in range(2):
            parts.append(found[pl.ds(2*h+o,PTS,stride=4),:].astype(BF)*mask[:,h*NG:(h+1)*NG])
    got=jnp.dot(jnp.concatenate(parts,axis=1),pick[...],preferred_element_type=jnp.float32)
    rows_out[...]=(got[:ROWS]*weight[...]).astype(BF)
    cols_out[...]=got[ROWS:].astype(BF)

def point_lists(g_index, slab_index, n_pair,n_grow,n_gcol,grow_at,gcol_at):
    rc=g_index.shape[0]//(n_pair*n_grow*n_gcol)
    cc=slab_index.shape[0]//(n_pair*n_grow*n_gcol)
    row_ids=g_index.reshape(n_pair,n_grow,n_gcol,rc)[:,grow_at,gcol_at]
    row_ids=jnp.pad(row_ids,((0,0),(0,NG-rc)),mode="edge")
    row_ids=jnp.transpose(row_ids.reshape(n_pair,2,64),(0,2,1)).reshape(ROWS,2)
    col_ids=slab_index.reshape(n_gcol,n_pair,n_grow,cc)[gcol_at,:,grow_at]
    col_ids=jnp.transpose(col_ids.reshape(2,COLS),(1,0))
    return jnp.concatenate([row_ids,col_ids],axis=0)

def stage_c(moved, ids, weight):
    q1=ids//(NG*NG); q2=ids//NG%QW; w=ids%PL
    place=((w*8+q2//4)*256+2*q1).reshape(-1)
    lane=jnp.arange(NG,dtype=jnp.int32)//PAIRS
    mask=((q2%4)[:,:,None]==lane).astype(BF).reshape(PTS,2*NG)
    wl=jnp.tile(weight,4).reshape(1,NG)
    t1,lp,pick=tables_c()
    vm=pl.BlockSpec(memory_space=pltpu.VMEM)
    return pl.pallas_call(kern_c,
        in_specs=[pl.BlockSpec(memory_space=pltpu.SMEM)]+[vm,vm,pl.BlockSpec(memory_space=pltpu.HBM),vm,vm,vm],
        out_specs=[vm,vm],
        out_shape=[jax.ShapeDtypeStruct((ROWS,NG),BF),jax.ShapeDtypeStruct((COLS,NG),BF)],
        scratch_shapes=[pltpu.VMEM((PL*8*256,NG),jnp.float32),pltpu.VMEM((4*PTS,NG),jnp.float32),pltpu.VMEM((1024,1024),BF),pltpu.SemaphoreType.DMA],
        compiler_params=pltpu.CompilerParams(vmem_limit_bytes=48*2**20),
        name="last_transform")(place,moved,t1,lp,pick,mask,wl)

def tables_d():
    q=np.zeros((2,2,2,PAIRS,2,2,2,2,PAIRS))
    for b in range(2):
        for h in range(2):
            for p in range(PAIRS):
                q[b,h,0,p,h,0,b,0,p]=1
                q[b,h,1,p,h,0,b,1,p]=1
                q[b,h,1,p,h,1,b,0,p]=1
                q[b,h,0,p,h,1,b,1,p]=-1
    return np.asarray(q.reshape(256,512),np.float32).astype(ml_dtypes.bfloat16)

def kern_d(order, rows, cols, turn, out, slab):
    @pl.when(pl.program_id(0) == 0)
    def _():
        for pp in range(4):
            a=cols[2*pp].astype(jnp.float32)
            b=cols[2*pp+1].astype(jnp.float32)
            for h in range(2):
                v=jnp.concatenate([a[:,h*64:(h+1)*64],b[:,h*64:(h+1)*64]],axis=1)
                v=jnp.concatenate([v[(g*4+pb)*8:(g*4+pb+1)*8] for pb in range(4) for g in range(8)],axis=0)
                slab[h*256:(h+1)*256,pp*NG:(pp+1)*NG]=v.astype(BF)
    turned=[]
    for pp in range(4):
        pair=jnp.concatenate([rows[0,order[4+2*pp+k]] for k in range(2)],axis=1)
        turned.append(jnp.dot(pair,turn[...],preferred_element_type=jnp.float32).astype(BF))
    lhs=jnp.concatenate([jnp.concatenate([t[:,k*NG:(k+1)*NG] for t in turned],axis=1) for k in range(4)],axis=0)
    z=lax.dot_general(lhs,slab[...],NT,preferred_element_type=jnp.float32)
    for hr in range(2):
        n=64 if hr==0 else 56
        for o in range(2):
            k=hr*2+o
            out[o,0,64*hr:64*hr+n,:]=z[k*64:k*64+n]

def stage_d(order, rows, cols):
    return pl.pallas_call(kern_d,
        grid_spec=pltpu.PrefetchScalarGridSpec(num_scalar_prefetch=1,grid=(4,),
            in_specs=[pl.BlockSpec((1,8,64,NG),lambda c,o:(o[c],0,0,0)),
                pl.BlockSpec((8,256,NG),lambda c,o:(0,0,0)),pl.BlockSpec((256,512),lambda c,o:(0,0))],
            out_specs=pl.BlockSpec((2,1,120,512),lambda c,o:(0,c,0,0)),
            scratch_shapes=[pltpu.VMEM((512,512),BF)]),
        out_shape=jax.ShapeDtypeStruct((2,4,120,512),jnp.float32),
        compiler_params=pltpu.CompilerParams(vmem_limit_bytes=32*2**20),
        name="pair_sums")(order,rows,cols,tables_d()).reshape(2,480,512)

def at(x, k, axis):
    return lax.dynamic_index_in_dim(x, k, axis, False)


def spread_rows(rows, pair_at, gcol_at):
    x_at, y_at = pair_at % 4, pair_at // 4
    both = ("pair", "gcol")
    got = [at(rows, x_at, 1)]
    for d in range(1, 4):
        perm = [(y * 4 + x, y * 4 + (x + d) % 4) for y in range(2) for x in range(4)]
        got.append(lax.ppermute(at(rows, (x_at + d) % 4, 1), "pair", perm))
    got = jnp.stack(got, axis=1)
    own, other = at(got, y_at, 0), at(got, 1 - y_at, 0)

    def swap(block, flip_pair, flip_gcol):
        return lax.ppermute(block, both, [(k, k ^ (flip_pair * 4 + flip_gcol)) for k in range(32)])

    block = jnp.stack([own, swap(other, 4, 0), swap(own, 0, 2), swap(other, 4, 2)]).reshape(2, 8, 64, NG)
    return jnp.concatenate([block, swap(block, 0, 1)])


def on_device(valence, conduction, pair_bands, e_val, e_cond, g_index, slab_index):
    n_pair = lax.axis_size("pair")
    n_grow = lax.axis_size("grow")
    n_gcol = lax.axis_size("gcol")
    pair_at = lax.axis_index("pair")
    grow_at = lax.axis_index("grow")
    gcol_at = lax.axis_index("gcol")
    bands = pair_bands.reshape(-1)
    part = stage_a(valence, conduction, bands)
    moved = lax.all_to_all(part.reshape(32, 8, 4096), ("grow", "gcol"), 0, 0, tiled=True)
    ids = point_lists(g_index, slab_index, n_pair, n_grow, n_gcol, grow_at, gcol_at)
    gaps = jnp.take(e_val, bands) - e_cond[0]
    weight = 2.0 / (gaps * math.sqrt(PAIRS * n_pair))
    rows, cols = stage_c(moved.reshape(256, 4096), ids, weight)
    cols = jnp.broadcast_to(cols[None], (64, COLS, NG))
    cols = lax.all_to_all(cols, ("pair", "grow"), 0, 0, tiled=True).reshape(8, 256, NG)
    rows = spread_rows(rows.reshape(2, 4, 64, NG), pair_at, gcol_at)
    c = jnp.arange(4, dtype=jnp.int32)
    blocks = (c % 2 ^ gcol_at % 2) * 2 + (c // 2 ^ gcol_at // 2)
    p = jnp.arange(8, dtype=jnp.int32)
    places = (p // 4 ^ pair_at // 4) * 4 + (pair_at - p) % 4
    return stage_d(jnp.concatenate([blocks, places]).astype(jnp.int32), rows, cols)


def solution(mesh):
    in_specs = (
        P(None, None, ("grow", "gcol"), None),
        P(None, "pair", ("grow", "gcol"), None),
        P("pair", None),
        P(),
        P("pair"),
        P(),
        P(),
    )
    out_specs = P(None, ("pair", "grow"), "gcol")
    return jax.shard_map(
        on_device, mesh=mesh, in_specs=in_specs, out_specs=out_specs, check_vma=False
    )
```

```python
import math
import numpy as np
import ml_dtypes
import jax
import jax.numpy as jnp
from jax import lax
from jax.sharding import PartitionSpec as P
from jax.experimental import pallas as pl
from jax.experimental.pallas import tpu as pltpu
BF=jnp.bfloat16
VM_A=62
CH=64
Q=4
NG=128; GR=8; GC=4; PL=4; QW=32; PAIRS=32; J=4
NT=(((1,),(1,)),((),()))
NN=(((1,),(0,)),((),()))

def cs(freq,pos):
    ph=(freq[:,None]*pos[None,:])%NG
    ang=ph.astype(np.float64)*(2*math.pi/NG)
    return np.cos(ang)/math.sqrt(NG), np.sin(ang)/math.sqrt(NG)

def tables():
    ar=np.arange(NG)
    c,w,g=np.meshgrid(np.arange(GC),np.arange(PL),np.arange(GR),indexing="ij")
    q3=((g*GC+c)*PL+w).reshape(-1)
    co,si=cs(q3,ar)
    t3=np.block([[co,si],[-si,co]])
    t2=np.zeros((GC,2,NG,2,J,QW))
    for cc in range(GC):
        co,si=cs(cc*QW+np.arange(QW),ar)
        t2[cc,0,:,0]=co.T[:,None]
        t2[cc,1,:,0]=si.T[:,None]
        t2[cc,0,:,1]=-si.T[:,None]
        t2[cc,1,:,1]=co.T[:,None]
    t2=t2.reshape(GC,2*NG,2*J*QW)
    perm=np.zeros((256,256))
    for cc in range(GC):
        for s in range(PL):
            for o in range(2):
                for g_ in range(GR):
                    perm[((g_*GC+cc)*PL+s)*2+o, ((cc*PL+s)*2+o)*GR+g_]=1
    return [np.asarray(t,np.float32).astype(ml_dtypes.bfloat16) for t in (t3,t2,perm)]

def kern_a(bands, val, cnd, t3, t2_hbm, perm_hbm, out, vbuf, dens, third, cond, t2_all, t2, perm, sems, vsems):
    step = pl.program_id(0)
    first = step == 0
    loads = [pltpu.make_async_copy(a, b, sems.at[k]) for k, (a, b) in enumerate(((t2_hbm, t2_all), (perm_hbm, perm)))]

    def band_load(k):
        return pltpu.make_async_copy(val.at[:, bands[k]], vbuf.at[k], vsems.at[k])

    @pl.when(first)
    def _():
        for k in range(Q*J):
            band_load(k).start()
        for load in loads:
            load.start()
        cond[...] = cnd[...].astype(jnp.float32)

    @pl.when(step < PAIRS//(Q*J) - 1)
    def _():
        for k in range(Q*J):
            band_load((step+1)*Q*J+k).start()

    for j in range(Q*J):
        k = step*Q*J+j
        band_load(k).wait()
        for r in range(0, NG*PL, CH):
            cr = cond[0, r:r+CH]
            ci = cond[1, r:r+CH]
            vr = vbuf[k, 0, r:r+CH].astype(jnp.float32)
            vi = vbuf[k, 1, r:r+CH].astype(jnp.float32)
            dens[j, 0, r:r+CH] = vr*cr+vi*ci
            dens[j, 1, r:r+CH] = vr*ci-vi*cr
    for j in range(Q*J):
        for sp in range(PL//2):
            rows = []
            for s in (2*sp, 2*sp+1):
                rows.append(jnp.concatenate([dens[j, i, pl.ds(s, NG, stride=PL), :].astype(BF) for i in range(2)], axis=1))
            d = jnp.concatenate(rows, axis=0)
            th = lax.dot_general(t3[...], d, NT, preferred_element_type=jnp.float32)
            third[j, sp] = th.astype(BF)

    @pl.when(first)
    def _():
        for load in loads:
            load.wait()
        part = lax.broadcasted_iota(jnp.int32, (2*NG, 2*J*QW), 1) // QW % J
        for c in range(GC):
            for j in range(J):
                t2[c, j*2*NG:(j+1)*2*NG] = jnp.where(part == j, t2_all[c].astype(jnp.float32), 0.0).astype(BF)

    ys=[]
    for c in range(GC):
        lhs=[]
        for q in range(Q):
            for s in range(PL):
                lhs.append(jnp.concatenate([third[q*J+j,s//2,i*NG+c*QW:i*NG+(c+1)*QW,(s%2)*NG:(s%2+1)*NG] for j in range(J) for i in range(2)],axis=1))
        lhs=jnp.concatenate(lhs,axis=0)
        ys.append(jnp.dot(lhs,t2[c],preferred_element_type=jnp.float32))
    for q in range(Q):
        for wp in range(PL//2):
            cols=[]
            for w in (2*wp,2*wp+1):
                pieces=[ys[c][(q*PL+s)*QW+w*GR:(q*PL+s)*QW+(w+1)*GR,o*NG:(o+1)*NG] for c in range(GC) for s in range(PL) for o in range(2)]
                cols.append(jnp.concatenate(pieces,axis=0).astype(BF))
            y=jnp.concatenate(cols,axis=1)
            out[:,(q*2+wp)*256:(q*2+wp+1)*256]=jnp.dot(perm[...],y,preferred_element_type=jnp.float32).astype(BF)

def stage_a(valence, cond, bands):
    nval=valence.shape[1]
    v=jnp.transpose(valence.reshape(2,nval,PL,NG,NG),(0,1,3,2,4)).reshape(2,nval,NG*PL,NG)
    cf=jnp.transpose(cond.reshape(2,PL,NG,NG),(0,2,1,3)).reshape(2,NG*PL,NG)
    t3,t2,perm=tables()
    full=lambda shape: pl.BlockSpec(shape,lambda q,b:(0,)*len(shape))
    return pl.pallas_call(kern_a,
        grid_spec=pltpu.PrefetchScalarGridSpec(num_scalar_prefetch=1,grid=(bands.shape[0]//(Q*J),),
            in_specs=[pl.BlockSpec(memory_space=pltpu.HBM),full((2,NG*PL,NG)),full((256,256))]+[pl.BlockSpec(memory_space=pltpu.HBM)]*2,
            out_specs=pl.BlockSpec((256,512*Q),lambda q,b:(0,q)),
            scratch_shapes=[pltpu.VMEM((PAIRS,2,NG*PL,NG),BF),pltpu.VMEM((Q*J,2,NG*PL,NG),jnp.float32),pltpu.VMEM((Q*J,PL//2,256,256),BF),pltpu.VMEM((2,NG*PL,NG),jnp.float32),
                pltpu.VMEM((GC,256,256),BF),pltpu.VMEM((GC,1024,256),BF),pltpu.VMEM((256,256),BF),pltpu.SemaphoreType.DMA((2,)),pltpu.SemaphoreType.DMA((PAIRS,))]),
        out_shape=jax.ShapeDtypeStruct((256,bands.shape[0]//J*512),BF),
        compiler_params=pltpu.CompilerParams(vmem_limit_bytes=VM_A*2**20),
        name="partial_transform")(bands,v,cf,t3,t2,perm)

ROWS=GR*64; COLS=32; COPIES=64; PTS=ROWS+COLS

def tables_c():
    ar=np.arange(NG)
    co,si=cs(ar,ar)
    t1=np.zeros((NG,2,NG,2))
    t1[:,0,:,0]=co; t1[:,0,:,1]=si; t1[:,1,:,0]=-si; t1[:,1,:,1]=co
    t1=t1.reshape(256,256)
    pick=np.zeros((2,2,4,PAIRS,2,2,PAIRS))
    for h in range(2):
        for o in range(2):
            for p in range(PAIRS):
                pick[h,o,:,p,h,o,p]=1
    pick=pick.reshape(512,128)
    return [np.asarray(t,np.float32).astype(ml_dtypes.bfloat16) for t in (t1,pick)]

def kern_c(place, x, t1, lp, pick, mask, weight, rows_out, cols_hbm, field, found, cols, sem):
    for w in range(PL):
        xw=jnp.concatenate([x[:,(q*PL+w)*NG:(q*PL+w+1)*NG] for q in range(8)],axis=1)
        e=jnp.dot(t1[...],xw,preferred_element_type=jnp.float32).astype(BF)
        f=jnp.dot(e,lp[...],preferred_element_type=jnp.float32)
        for t in range(8):
            field[(w*8+t)*256:(w*8+t+1)*256,:]=f[:,t*NG:(t+1)*NG]

    def find(first, last):
        def body(r,carry):
            for h in range(2):
                at=pl.multiple_of(place[2*r+h],2)
                found[pl.ds(pl.multiple_of(4*r+2*h,2),2),:]=field[pl.ds(at,2),:]
            return carry
        lax.fori_loop(first,last,body,0,unroll=8)
        parts=[]
        for h in range(2):
            for o in range(2):
                parts.append(found[pl.ds(4*first+2*h+o,last-first,stride=4),:].astype(BF)*mask[first:last,h*NG:(h+1)*NG])
        return jnp.dot(jnp.concatenate(parts,axis=1),pick[...],preferred_element_type=jnp.float32)

    cols[...]=jnp.broadcast_to(find(ROWS,PTS).astype(BF)[None],(COPIES,COLS,NG))
    send=pltpu.make_async_copy(cols,cols_hbm,sem)
    send.start()
    rows_out[...]=(find(0,ROWS)*weight[...]).astype(BF)
    send.wait()

def point_lists(g_index, slab_index, n_pair,n_grow,n_gcol,grow_at,gcol_at):
    rc=g_index.shape[0]//(n_pair*n_grow*n_gcol)
    cc=slab_index.shape[0]//(n_pair*n_grow*n_gcol)
    row_ids=g_index.reshape(n_pair,n_grow,n_gcol,rc)[:,grow_at,gcol_at]
    row_ids=jnp.pad(row_ids,((0,0),(0,NG-rc)),mode="edge")
    row_ids=jnp.transpose(row_ids.reshape(n_pair,2,64),(0,2,1)).reshape(ROWS,2)
    col_ids=slab_index.reshape(n_gcol,n_pair,n_grow,cc)[gcol_at,:,grow_at]
    col_ids=jnp.transpose(col_ids.reshape(2,COLS),(1,0))
    return jnp.concatenate([row_ids,col_ids],axis=0)

def stage_c(moved, ids, weight):
    q1=ids//(NG*NG); q2=ids//NG%QW; w=ids%PL
    place=((w*8+q2//4)*256+2*q1).reshape(-1)
    lane=jnp.arange(NG,dtype=jnp.int32)//PAIRS
    mask=((q2%4)[:,:,None]==lane).astype(BF).reshape(PTS,2*NG)
    wl=jnp.tile(weight,4).reshape(1,NG)
    t1,pick=tables_c()
    r=lax.broadcasted_iota(jnp.int32,(1024,1024),0)
    l=lax.broadcasted_iota(jnp.int32,(1024,1024),1)
    lp=((r//QW==l%PAIRS)&(r%QW==l//PAIRS)).astype(BF)
    vm=pl.BlockSpec(memory_space=pltpu.VMEM)
    return pl.pallas_call(kern_c,
        in_specs=[pl.BlockSpec(memory_space=pltpu.SMEM)]+[vm]*6,
        out_specs=[vm,pl.BlockSpec(memory_space=pltpu.HBM)],
        out_shape=[jax.ShapeDtypeStruct((ROWS,NG),BF),jax.ShapeDtypeStruct((COPIES,COLS,NG),BF)],
        scratch_shapes=[pltpu.VMEM((PL*8*256,NG),jnp.float32),pltpu.VMEM((4*PTS,NG),jnp.float32),pltpu.VMEM((COPIES,COLS,NG),BF),pltpu.SemaphoreType.DMA],
        compiler_params=pltpu.CompilerParams(vmem_limit_bytes=40*2**20),
        name="last_transform")(place,moved,t1,lp,pick,mask,wl)

def tables_d():
    q=np.zeros((2,2,2,PAIRS,2,2,2,2,PAIRS))
    for b in range(2):
        for h in range(2):
            for p in range(PAIRS):
                q[b,h,0,p,h,0,b,0,p]=1
                q[b,h,1,p,h,0,b,1,p]=1
                q[b,h,1,p,h,1,b,0,p]=1
                q[b,h,0,p,h,1,b,1,p]=-1
    return np.asarray(q.reshape(256,512),np.float32).astype(ml_dtypes.bfloat16)

def kern_d(order, rows, cols, turn, out, slab):
    @pl.when(pl.program_id(0) == 0)
    def _():
        for pp in range(4):
            a=cols[2*pp].astype(jnp.float32)
            b=cols[2*pp+1].astype(jnp.float32)
            for h in range(2):
                v=jnp.concatenate([a[:,h*64:(h+1)*64],b[:,h*64:(h+1)*64]],axis=1)
                v=jnp.concatenate([v[(g*4+pb)*8:(g*4+pb+1)*8] for pb in range(4) for g in range(8)],axis=0)
                slab[h*256:(h+1)*256,pp*NG:(pp+1)*NG]=v.astype(BF)
    turned=[]
    for pp in range(4):
        pair=jnp.concatenate([rows[0,order[4+2*pp+k]] for k in range(2)],axis=1)
        turned.append(jnp.dot(pair,turn[...],preferred_element_type=jnp.float32).astype(BF))
    lhs=jnp.concatenate([jnp.concatenate([t[:,k*NG:(k+1)*NG] for t in turned],axis=1) for k in range(4)],axis=0)
    z=lax.dot_general(lhs,slab[...],NT,preferred_element_type=jnp.float32)
    for hr in range(2):
        n=64 if hr==0 else 56
        for o in range(2):
            k=hr*2+o
            out[o,0,64*hr:64*hr+n,:]=z[k*64:k*64+n]

def stage_d(order, rows, cols):
    return pl.pallas_call(kern_d,
        grid_spec=pltpu.PrefetchScalarGridSpec(num_scalar_prefetch=1,grid=(4,),
            in_specs=[pl.BlockSpec((1,8,64,NG),lambda c,o:(o[c],0,0,0)),
                pl.BlockSpec((8,256,NG),lambda c,o:(0,0,0)),pl.BlockSpec((256,512),lambda c,o:(0,0))],
            out_specs=pl.BlockSpec((2,1,120,512),lambda c,o:(0,c,0,0)),
            scratch_shapes=[pltpu.VMEM((512,512),BF)]),
        out_shape=jax.ShapeDtypeStruct((2,4,120,512),jnp.float32),
        compiler_params=pltpu.CompilerParams(vmem_limit_bytes=32*2**20),
        name="pair_sums")(order,rows,cols,tables_d()).reshape(2,480,512)

def at(x, k, axis):
    return lax.dynamic_index_in_dim(x, k, axis, False)


def spread_rows(rows, pair_at, gcol_at):
    x_at, y_at = pair_at % 4, pair_at // 4
    both = ("pair", "gcol")
    got = [at(rows, x_at, 1)]
    for d in range(1, 4):
        perm = [(y * 4 + x, y * 4 + (x + d) % 4) for y in range(2) for x in range(4)]
        got.append(lax.ppermute(at(rows, (x_at + d) % 4, 1), "pair", perm))
    got = jnp.stack(got, axis=1)
    own, other = at(got, y_at, 0), at(got, 1 - y_at, 0)

    def swap(block, flip_pair, flip_gcol):
        return lax.ppermute(block, both, [(k, k ^ (flip_pair * 4 + flip_gcol)) for k in range(32)])

    block = jnp.stack([own, swap(other, 4, 0), swap(own, 0, 2), swap(other, 4, 2)]).reshape(2, 8, 64, NG)
    return jnp.concatenate([block, swap(block, 0, 1)])


def on_device(valence, conduction, pair_bands, e_val, e_cond, g_index, slab_index):
    n_pair = lax.axis_size("pair")
    n_grow = lax.axis_size("grow")
    n_gcol = lax.axis_size("gcol")
    pair_at = lax.axis_index("pair")
    grow_at = lax.axis_index("grow")
    gcol_at = lax.axis_index("gcol")
    bands = pair_bands.reshape(-1)
    part = stage_a(valence, conduction, bands)
    moved = lax.all_to_all(part.reshape(32, 8, 4096), ("grow", "gcol"), 0, 0, tiled=True)
    ids = point_lists(g_index, slab_index, n_pair, n_grow, n_gcol, grow_at, gcol_at)
    gaps = jnp.take(e_val, bands) - e_cond[0]
    weight = 2.0 / (gaps * math.sqrt(PAIRS * n_pair))
    rows, cols = stage_c(moved.reshape(256, 4096), ids, weight)
    cols = lax.all_to_all(cols, ("pair", "grow"), 0, 0, tiled=True).reshape(8, 256, NG)
    rows = spread_rows(rows.reshape(2, 4, 64, NG), pair_at, gcol_at)
    c = jnp.arange(4, dtype=jnp.int32)
    blocks = (c % 2 ^ gcol_at % 2) * 2 + (c // 2 ^ gcol_at // 2)
    p = jnp.arange(8, dtype=jnp.int32)
    places = (p // 4 ^ pair_at // 4) * 4 + (pair_at - p) % 4
    return stage_d(jnp.concatenate([blocks, places]).astype(jnp.int32), rows, cols)


def solution(mesh):
    in_specs = (
        P(None, None, ("grow", "gcol"), None),
        P(None, "pair", ("grow", "gcol"), None),
        P("pair", None),
        P(),
        P("pair"),
        P(),
        P(),
    )
    out_specs = P(None, ("pair", "grow"), "gcol")
    return jax.shard_map(
        on_device, mesh=mesh, in_specs=in_specs, out_specs=out_specs, check_vma=False
    )
```

```python
import math
import numpy as np
import ml_dtypes
import jax
import jax.numpy as jnp
from jax import lax
from jax.sharding import PartitionSpec as P
from jax.experimental import pallas as pl
from jax.experimental.pallas import tpu as pltpu
BF=jnp.bfloat16
VM_A=62
CH=64
Q=4
NG=128; GR=8; GC=4; PL=4; QW=32; PAIRS=32; J=4
NT=(((1,),(1,)),((),()))
NN=(((1,),(0,)),((),()))

def cs(freq,pos):
    ph=(freq[:,None]*pos[None,:])%NG
    ang=ph.astype(np.float64)*(2*math.pi/NG)
    return np.cos(ang)/math.sqrt(NG), np.sin(ang)/math.sqrt(NG)

def tables():
    ar=np.arange(NG)
    c,w,g=np.meshgrid(np.arange(GC),np.arange(PL),np.arange(GR),indexing="ij")
    q3=((g*GC+c)*PL+w).reshape(-1)
    co,si=cs(q3,ar)
    t3=np.block([[co,si],[-si,co]])
    t2=np.zeros((GC,2,NG,2,QW,J))
    for cc in range(GC):
        co,si=cs(cc*QW+np.arange(QW),ar)
        t2[cc,0,:,0]=co.T[:,:,None]
        t2[cc,1,:,0]=si.T[:,:,None]
        t2[cc,0,:,1]=-si.T[:,:,None]
        t2[cc,1,:,1]=co.T[:,:,None]
    t2=t2.reshape(GC,2*NG,2*J*QW)
    perm=np.zeros((256,256))
    for cc in range(GC):
        for s in range(PL):
            for o in range(2):
                for g_ in range(GR):
                    perm[((g_*GC+cc)*PL+s)*2+o, ((cc*PL+s)*2+o)*GR+g_]=1
    return [np.asarray(t,np.float32).astype(ml_dtypes.bfloat16) for t in (t3,t2,perm)]

def kern_a(bands, val, cnd_hbm, t3_hbm, t2_hbm, perm_hbm, out, vbuf, dens, third, cnd, cond, t3, t2_all, t2, perm, sems, vsems):
    step = pl.program_id(0)
    first = step == 0
    loads = [pltpu.make_async_copy(a, b, sems.at[k]) for k, (a, b) in enumerate(((cnd_hbm, cnd), (t3_hbm, t3), (t2_hbm, t2_all), (perm_hbm, perm)))]

    def band_load(k):
        return pltpu.make_async_copy(val.at[:, bands[k]], vbuf.at[k], vsems.at[k])

    @pl.when(first)
    def _():
        loads[0].start()
        band_load(0).start()
        loads[1].start()
        for k in range(1, Q*J):
            band_load(k).start()
        loads[2].start()
        loads[3].start()
        loads[0].wait()
        cond[...] = cnd[...].astype(jnp.float32)
        loads[1].wait()

    @pl.when(step < PAIRS//(Q*J) - 1)
    def _():
        for k in range(Q*J):
            band_load((step+1)*Q*J+k).start()

    for j in range(Q*J):
        k = step*Q*J+j
        band_load(k).wait()
        for r in range(0, NG*PL, CH):
            cr = cond[0, r:r+CH]
            ci = cond[1, r:r+CH]
            vr = vbuf[k, 0, r:r+CH].astype(jnp.float32)
            vi = vbuf[k, 1, r:r+CH].astype(jnp.float32)
            dens[j, 0, r:r+CH] = vr*cr+vi*ci
            dens[j, 1, r:r+CH] = vr*ci-vi*cr
    for j in range(Q*J):
        for sp in range(PL//2):
            rows = []
            for s in (2*sp, 2*sp+1):
                rows.append(jnp.concatenate([dens[j, i, pl.ds(s, NG, stride=PL), :].astype(BF) for i in range(2)], axis=1))
            d = jnp.concatenate(rows, axis=0)
            th = lax.dot_general(t3[...], d, NT, preferred_element_type=jnp.float32)
            third[j, sp] = th.astype(BF)

    @pl.when(first)
    def _():
        loads[2].wait()
        loads[3].wait()
        part = lax.broadcasted_iota(jnp.int32, (2*NG, 2*J*QW), 1) % J
        for c in range(GC):
            for j in range(J):
                t2[c, j*2*NG:(j+1)*2*NG] = jnp.where(part == j, t2_all[c].astype(jnp.float32), 0.0).astype(BF)

    ys=[]
    for c in range(GC):
        lhs=[]
        for q in range(Q):
            for s in range(PL):
                lhs.append(jnp.concatenate([third[q*J+j,s//2,i*NG+c*QW:i*NG+(c+1)*QW,(s%2)*NG:(s%2+1)*NG] for j in range(J) for i in range(2)],axis=1))
        lhs=jnp.concatenate(lhs,axis=0)
        ys.append(jnp.dot(lhs,t2[c],preferred_element_type=jnp.float32))
    for q in range(Q):
        for wp in range(PL//2):
            cols=[]
            for w in (2*wp,2*wp+1):
                pieces=[ys[c][(q*PL+s)*QW+w*GR:(q*PL+s)*QW+(w+1)*GR,o*NG:(o+1)*NG] for c in range(GC) for s in range(PL) for o in range(2)]
                cols.append(jnp.concatenate(pieces,axis=0).astype(BF))
            y=jnp.concatenate(cols,axis=1)
            out[:,(q*2+wp)*256:(q*2+wp+1)*256]=jnp.dot(perm[...],y,preferred_element_type=jnp.float32).astype(BF)


def stage_a(valence, cond, bands):
    nval=valence.shape[1]
    v=jnp.transpose(valence.reshape(2,nval,PL,NG,NG),(0,1,3,2,4)).reshape(2,nval,NG*PL,NG)
    cf=jnp.transpose(cond.reshape(2,PL,NG,NG),(0,2,1,3)).reshape(2,NG*PL,NG)
    t3,t2,perm=tables()
    return pl.pallas_call(kern_a,
        grid_spec=pltpu.PrefetchScalarGridSpec(num_scalar_prefetch=1,grid=(bands.shape[0]//(Q*J),),
            in_specs=[pl.BlockSpec(memory_space=pltpu.HBM)]*5,
            out_specs=pl.BlockSpec((256,512*Q),lambda q,b:(0,q)),
            scratch_shapes=[pltpu.VMEM((PAIRS,2,NG*PL,NG),BF),pltpu.VMEM((Q*J,2,NG*PL,NG),jnp.float32),pltpu.VMEM((Q*J,PL//2,256,256),BF),pltpu.VMEM((2,NG*PL,NG),BF),pltpu.VMEM((2,NG*PL,NG),jnp.float32),pltpu.VMEM((256,256),BF),
                pltpu.VMEM((GC,256,256),BF),pltpu.VMEM((GC,1024,256),BF),pltpu.VMEM((256,256),BF),
                pltpu.SemaphoreType.DMA((4,)),pltpu.SemaphoreType.DMA((PAIRS,))]),
        out_shape=jax.ShapeDtypeStruct((256,bands.shape[0]//J*512),BF),
        compiler_params=pltpu.CompilerParams(vmem_limit_bytes=VM_A*2**20),
        name="partial_transform")(bands,v,cf,t3,t2,perm)

ROWS=GR*64; COLS=32; COPIES=64; PTS=ROWS+COLS

def tables_c():
    ar=np.arange(NG)
    co,si=cs(ar,ar)
    t1=np.zeros((NG,2,NG,2))
    t1[:,0,:,0]=co; t1[:,0,:,1]=si; t1[:,1,:,0]=-si; t1[:,1,:,1]=co
    t1=t1.reshape(256,256)
    pick=np.zeros((2,2,8,4,J,2,2,8,J))
    for h in range(2):
        for o in range(2):
            for q in range(8):
                for j in range(J):
                    pick[h,o,q,:,j,h,o,q,j]=1
    pick=pick.reshape(512,128)
    return [np.asarray(t,np.float32).astype(ml_dtypes.bfloat16) for t in (t1,pick)]

def kern_c(place, x, t1, pick, mask, weight, rows_out, cols_hbm, field, found, cols, sem):
    group=lax.broadcasted_iota(jnp.int32,(256,NG),1)//16
    for w in range(PL):
        xw=jnp.concatenate([x[:,(q*PL+w)*NG:(q*PL+w+1)*NG] for q in range(8)],axis=1)
        f=jnp.dot(t1[...],xw,preferred_element_type=jnp.float32).astype(BF).astype(jnp.float32)
        f=[f[:,t*NG:(t+1)*NG] for t in range(8)]
        for k in (1,2,4):
            low=group//k%2==0
            f=[jnp.where(low,f[t],pltpu.roll(f[t^k],16*k,1)) if t&k==0 else jnp.where(low,pltpu.roll(f[t^k],NG-16*k,1),f[t]) for t in range(8)]
        for t in range(8):
            field[(w*8+t)*256:(w*8+t+1)*256,:]=f[t]

    def find(first, last):
        def body(r,carry):
            for h in range(2):
                at=pl.multiple_of(place[2*r+h],2)
                found[pl.ds(pl.multiple_of(4*r+2*h,2),2),:]=field[pl.ds(at,2),:]
            return carry
        lax.fori_loop(first,last,body,0,unroll=8)
        parts=[]
        for h in range(2):
            for o in range(2):
                parts.append(found[pl.ds(4*first+2*h+o,last-first,stride=4),:].astype(BF)*mask[first:last,h*NG:(h+1)*NG])
        return jnp.dot(jnp.concatenate(parts,axis=1),pick[...],preferred_element_type=jnp.float32)

    cols[...]=jnp.broadcast_to(find(ROWS,PTS).astype(BF)[None],(COPIES,COLS,NG))
    send=pltpu.make_async_copy(cols,cols_hbm,sem)
    send.start()
    rows_out[...]=(find(0,ROWS)*weight[...]).astype(BF)
    send.wait()

def point_lists(g_index, slab_index, n_pair,n_grow,n_gcol,grow_at,gcol_at):
    rc=g_index.shape[0]//(n_pair*n_grow*n_gcol)
    cc=slab_index.shape[0]//(n_pair*n_grow*n_gcol)
    row_ids=g_index.reshape(n_pair,n_grow,n_gcol,rc)[:,grow_at,gcol_at]
    row_ids=jnp.pad(row_ids,((0,0),(0,NG-rc)),mode="edge")
    row_ids=jnp.transpose(row_ids.reshape(n_pair,2,64),(0,2,1)).reshape(ROWS,2)
    col_ids=slab_index.reshape(n_gcol,n_pair,n_grow,cc)[gcol_at,:,grow_at]
    col_ids=jnp.transpose(col_ids.reshape(2,COLS),(1,0))
    return jnp.concatenate([row_ids,col_ids],axis=0)

def stage_c(moved, ids, weight):
    q1=ids//(NG*NG); q2=ids//NG%QW; w=ids%PL
    place=((w*8+q2//4)*256+2*q1).reshape(-1)
    lane=jnp.arange(NG,dtype=jnp.int32)//J%4
    mask=((q2%4)[:,:,None]==lane).astype(BF).reshape(PTS,2*NG)
    wl=jnp.tile(weight,4).reshape(1,NG)
    t1,pick=tables_c()
    vm=pl.BlockSpec(memory_space=pltpu.VMEM)
    return pl.pallas_call(kern_c,
        in_specs=[pl.BlockSpec(memory_space=pltpu.SMEM)]+[vm]*5,
        out_specs=[vm,pl.BlockSpec(memory_space=pltpu.HBM)],
        out_shape=[jax.ShapeDtypeStruct((ROWS,NG),BF),jax.ShapeDtypeStruct((COPIES,COLS,NG),BF)],
        scratch_shapes=[pltpu.VMEM((PL*8*256,NG),jnp.float32),pltpu.VMEM((4*PTS,NG),jnp.float32),pltpu.VMEM((COPIES,COLS,NG),BF),pltpu.SemaphoreType.DMA],
        compiler_params=pltpu.CompilerParams(vmem_limit_bytes=40*2**20),
        name="last_transform")(place,moved,t1,pick,mask,wl)

def tables_d():
    q=np.zeros((2,2,2,PAIRS,2,2,2,2,PAIRS))
    for b in range(2):
        for h in range(2):
            for p in range(PAIRS):
                q[b,h,0,p,h,0,b,0,p]=1
                q[b,h,1,p,h,0,b,1,p]=1
                q[b,h,1,p,h,1,b,0,p]=1
                q[b,h,0,p,h,1,b,1,p]=-1
    return np.asarray(q.reshape(256,512),np.float32).astype(ml_dtypes.bfloat16)

def kern_d(order, rows, cols, turn, out, slab):
    @pl.when(pl.program_id(0) == 0)
    def _():
        for pp in range(4):
            a=cols[2*pp].astype(jnp.float32)
            b=cols[2*pp+1].astype(jnp.float32)
            for h in range(2):
                v=jnp.concatenate([a[:,h*64:(h+1)*64],b[:,h*64:(h+1)*64]],axis=1)
                v=jnp.concatenate([v[(g*4+pb)*8:(g*4+pb+1)*8] for pb in range(4) for g in range(8)],axis=0)
                slab[h*256:(h+1)*256,pp*NG:(pp+1)*NG]=v.astype(BF)
    turned=[]
    for pp in range(4):
        pair=jnp.concatenate([rows[0,order[4+2*pp+k]] for k in range(2)],axis=1)
        turned.append(jnp.dot(pair,turn[...],preferred_element_type=jnp.float32).astype(BF))
    lhs=jnp.concatenate([jnp.concatenate([t[:,k*NG:(k+1)*NG] for t in turned],axis=1) for k in range(4)],axis=0)
    z=lax.dot_general(lhs,slab[...],NT,preferred_element_type=jnp.float32)
    for hr in range(2):
        n=64 if hr==0 else 56
        for o in range(2):
            k=hr*2+o
            out[o,0,64*hr:64*hr+n,:]=z[k*64:k*64+n]

def stage_d(order, rows, cols):
    return pl.pallas_call(kern_d,
        grid_spec=pltpu.PrefetchScalarGridSpec(num_scalar_prefetch=1,grid=(4,),
            in_specs=[pl.BlockSpec((1,8,64,NG),lambda c,o:(o[c],0,0,0)),
                pl.BlockSpec((8,256,NG),lambda c,o:(0,0,0)),pl.BlockSpec((256,512),lambda c,o:(0,0))],
            out_specs=pl.BlockSpec((2,1,120,512),lambda c,o:(0,c,0,0)),
            scratch_shapes=[pltpu.VMEM((512,512),BF)]),
        out_shape=jax.ShapeDtypeStruct((2,4,120,512),jnp.float32),
        compiler_params=pltpu.CompilerParams(vmem_limit_bytes=32*2**20),
        name="pair_sums")(order,rows,cols,tables_d()).reshape(2,480,512)

def at(x, k, axis):
    return lax.dynamic_index_in_dim(x, k, axis, False)


def spread_rows(rows, pair_at, gcol_at):
    x_at, y_at = pair_at % 4, pair_at // 4
    both = ("pair", "gcol")
    got = [at(rows, x_at, 1)]
    for d in range(1, 4):
        perm = [(y * 4 + x, y * 4 + (x + d) % 4) for y in range(2) for x in range(4)]
        got.append(lax.ppermute(at(rows, (x_at + d) % 4, 1), "pair", perm))
    got = jnp.stack(got, axis=1)
    own, other = at(got, y_at, 0), at(got, 1 - y_at, 0)

    def swap(block, flip_pair, flip_gcol):
        return lax.ppermute(block, both, [(k, k ^ (flip_pair * 4 + flip_gcol)) for k in range(32)])

    block = jnp.stack([own, swap(other, 4, 0), swap(own, 0, 2), swap(other, 4, 2)]).reshape(2, 8, 64, NG)
    return jnp.concatenate([block, swap(block, 0, 1)])


def on_device(valence, conduction, pair_bands, e_val, e_cond, g_index, slab_index):
    n_pair = lax.axis_size("pair")
    n_grow = lax.axis_size("grow")
    n_gcol = lax.axis_size("gcol")
    pair_at = lax.axis_index("pair")
    grow_at = lax.axis_index("grow")
    gcol_at = lax.axis_index("gcol")
    bands = pair_bands.reshape(-1)
    part = stage_a(valence, conduction, bands)
    moved = lax.all_to_all(part.reshape(32, 8, 4096), ("grow", "gcol"), 0, 0, tiled=True)
    ids = point_lists(g_index, slab_index, n_pair, n_grow, n_gcol, grow_at, gcol_at)
    gaps = jnp.take(e_val, bands) - e_cond[0]
    weight = 2.0 / (gaps * math.sqrt(PAIRS * n_pair))
    rows, cols = stage_c(moved.reshape(256, 4096), ids, weight)
    cols = lax.all_to_all(cols, ("pair", "grow"), 0, 0, tiled=True).reshape(8, 256, NG)
    rows = spread_rows(rows.reshape(2, 4, 64, NG), pair_at, gcol_at)
    c = jnp.arange(4, dtype=jnp.int32)
    blocks = (c % 2 ^ gcol_at % 2) * 2 + (c // 2 ^ gcol_at // 2)
    p = jnp.arange(8, dtype=jnp.int32)
    places = (p // 4 ^ pair_at // 4) * 4 + (pair_at - p) % 4
    return stage_d(jnp.concatenate([blocks, places]).astype(jnp.int32), rows, cols)


def solution(mesh):
    in_specs = (
        P(None, None, ("grow", "gcol"), None),
        P(None, "pair", ("grow", "gcol"), None),
        P("pair", None),
        P(),
        P("pair"),
        P(),
        P(),
    )
    out_specs = P(None, ("pair", "grow"), "gcol")
    return jax.shard_map(
        on_device, mesh=mesh, in_specs=in_specs, out_specs=out_specs, check_vma=False
    )
```

```python
import functools
import math
import numpy as np
import ml_dtypes
import jax
import jax.numpy as jnp
from jax import lax
from jax.sharding import PartitionSpec as P
from jax.experimental import pallas as pl
from jax.experimental.pallas import tpu as pltpu
BF=jnp.bfloat16
VM_A=62
CH=64
NG=128; GR=8; GC=4; PL=4; QW=32; PAIRS=32; J=4
NT=(((1,),(1,)),((),()))
NN=(((1,),(0,)),((),()))

def cs(freq,pos):
    ph=(freq[:,None]*pos[None,:])%NG
    ang=ph.astype(np.float64)*(2*math.pi/NG)
    return np.cos(ang)/math.sqrt(NG), np.sin(ang)/math.sqrt(NG)

def tables():
    ar=np.arange(NG)
    c,w,g=np.meshgrid(np.arange(GC),np.arange(PL),np.arange(GR),indexing="ij")
    q3=((g*GC+c)*PL+w).reshape(-1)
    co,si=cs(q3,ar)
    t3=np.block([[co,si],[-si,co]])
    t2=np.zeros((GC,2,NG,2,QW,J))
    for cc in range(GC):
        co,si=cs(cc*QW+np.arange(QW),ar)
        t2[cc,0,:,0]=co.T[:,:,None]
        t2[cc,1,:,0]=si.T[:,:,None]
        t2[cc,0,:,1]=-si.T[:,:,None]
        t2[cc,1,:,1]=co.T[:,:,None]
    t2=t2.reshape(GC,2*NG,2*J*QW)
    perm=np.zeros((256,256))
    for cc in range(GC):
        for s in range(PL):
            for o in range(2):
                for g_ in range(GR):
                    perm[((g_*GC+cc)*PL+s)*2+o, ((cc*PL+s)*2+o)*GR+g_]=1
    return [np.asarray(t,np.float32).astype(ml_dtypes.bfloat16) for t in (t3,t2,perm)]

def kern_a(Q, steps, bands, val, cnd_hbm, t3_hbm, t2_hbm, perm_hbm, out, vbuf, dens, third, cnd, cond, t3, t2_all, t2, perm, sems, vsems):
    step = pl.program_id(0)
    first = step == 0
    loads = [pltpu.make_async_copy(a, b, sems.at[k]) for k, (a, b) in enumerate(((cnd_hbm, cnd), (t3_hbm, t3), (t2_hbm, t2_all), (perm_hbm, perm)))]

    def band_load(k):
        return pltpu.make_async_copy(val.at[:, bands[k]], vbuf.at[k], vsems.at[k])

    @pl.when(first)
    def _():
        loads[0].start()
        band_load(0).start()
        loads[1].start()
        for k in range(1, Q*J):
            band_load(k).start()
        loads[2].start()
        loads[3].start()
        loads[0].wait()
        cond[...] = cnd[...].astype(jnp.float32)
        loads[1].wait()

    @pl.when(step < steps - 1)
    def _():
        for k in range(Q*J):
            band_load((step+1)*Q*J+k).start()

    for j in range(Q*J):
        k = step*Q*J+j
        band_load(k).wait()
        for r in range(0, NG*PL, CH):
            cr = cond[0, r:r+CH]
            ci = cond[1, r:r+CH]
            vr = vbuf[k, 0, r:r+CH].astype(jnp.float32)
            vi = vbuf[k, 1, r:r+CH].astype(jnp.float32)
            dens[j, 0, r:r+CH] = vr*cr+vi*ci
            dens[j, 1, r:r+CH] = vr*ci-vi*cr
    for j in range(Q*J):
        for sp in range(PL//2):
            rows = []
            for s in (2*sp, 2*sp+1):
                rows.append(jnp.concatenate([dens[j, i, pl.ds(s, NG, stride=PL), :].astype(BF) for i in range(2)], axis=1))
            d = jnp.concatenate(rows, axis=0)
            th = lax.dot_general(t3[...], d, NT, preferred_element_type=jnp.float32)
            third[j, sp] = th.astype(BF)

    @pl.when(first)
    def _():
        loads[2].wait()
        loads[3].wait()
        part = lax.broadcasted_iota(jnp.int32, (2*NG, 2*J*QW), 1) % J
        for c in range(GC):
            for j in range(J):
                t2[c, j*2*NG:(j+1)*2*NG] = jnp.where(part == j, t2_all[c].astype(jnp.float32), 0.0).astype(BF)

    ys=[]
    for c in range(GC):
        lhs=[]
        for q in range(Q):
            for s in range(PL):
                lhs.append(jnp.concatenate([third[q*J+j,s//2,i*NG+c*QW:i*NG+(c+1)*QW,(s%2)*NG:(s%2+1)*NG] for j in range(J) for i in range(2)],axis=1))
        lhs=jnp.concatenate(lhs,axis=0)
        ys.append(jnp.dot(lhs,t2[c],preferred_element_type=jnp.float32))
    for q in range(Q):
        for wp in range(PL//2):
            cols=[]
            for w in (2*wp,2*wp+1):
                pieces=[ys[c][(q*PL+s)*QW+w*GR:(q*PL+s)*QW+(w+1)*GR,o*NG:(o+1)*NG] for c in range(GC) for s in range(PL) for o in range(2)]
                cols.append(jnp.concatenate(pieces,axis=0).astype(BF))
            y=jnp.concatenate(cols,axis=1)
            out[:,(q*2+wp)*256:(q*2+wp+1)*256]=jnp.dot(perm[...],y,preferred_element_type=jnp.float32).astype(BF)


def stage_a(valence, cond, bands, Q=4):
    nval=valence.shape[1]
    v=jnp.transpose(valence.reshape(2,nval,PL,NG,NG),(0,1,3,2,4)).reshape(2,nval,NG*PL,NG)
    cf=jnp.transpose(cond.reshape(2,PL,NG,NG),(0,2,1,3)).reshape(2,NG*PL,NG)
    t3,t2,perm=tables()
    steps=bands.shape[0]//(Q*J)
    return pl.pallas_call(functools.partial(kern_a,Q,steps),
        grid_spec=pltpu.PrefetchScalarGridSpec(num_scalar_prefetch=1,grid=(steps,),
            in_specs=[pl.BlockSpec(memory_space=pltpu.HBM)]*5,
            out_specs=pl.BlockSpec((256,512*Q),lambda q,b:(0,q)),
            scratch_shapes=[pltpu.VMEM((PAIRS,2,NG*PL,NG),BF),pltpu.VMEM((Q*J,2,NG*PL,NG),jnp.float32),pltpu.VMEM((Q*J,PL//2,256,256),BF),pltpu.VMEM((2,NG*PL,NG),BF),pltpu.VMEM((2,NG*PL,NG),jnp.float32),pltpu.VMEM((256,256),BF),
                pltpu.VMEM((GC,256,256),BF),pltpu.VMEM((GC,1024,256),BF),pltpu.VMEM((256,256),BF),
                pltpu.SemaphoreType.DMA((4,)),pltpu.SemaphoreType.DMA((PAIRS,))]),
        out_shape=jax.ShapeDtypeStruct((256,bands.shape[0]//J*512),BF),
        compiler_params=pltpu.CompilerParams(vmem_limit_bytes=VM_A*2**20),
        name="partial_transform")(bands,v,cf,t3,t2,perm)

ROWS=GR*64; COLS=32; COPIES=64; PTS=ROWS+COLS

def tables_c():
    ar=np.arange(NG)
    co,si=cs(ar,ar)
    t1=np.zeros((NG,2,NG,2))
    t1[:,0,:,0]=co; t1[:,0,:,1]=si; t1[:,1,:,0]=-si; t1[:,1,:,1]=co
    t1=t1.reshape(256,256)
    pick=np.zeros((2,2,8,4,J,2,2,8,J))
    for h in range(2):
        for o in range(2):
            for q in range(8):
                for j in range(J):
                    pick[h,o,q,:,j,h,o,q,j]=1
    pick=pick.reshape(512,128)
    return [np.asarray(t,np.float32).astype(ml_dtypes.bfloat16) for t in (t1,pick)]

def kern_c(place, x, t1, pick, mask, weight, rows_out, cols_hbm, field, found, cols, sem):
    group=lax.broadcasted_iota(jnp.int32,(256,NG),1)//16
    for w in range(PL):
        xw=jnp.concatenate([x[:,(q*PL+w)*NG:(q*PL+w+1)*NG] for q in range(8)],axis=1)
        f=jnp.dot(t1[...],xw,preferred_element_type=jnp.float32).astype(BF).astype(jnp.float32)
        f=[f[:,t*NG:(t+1)*NG] for t in range(8)]
        for k in (1,2,4):
            low=group//k%2==0
            f=[jnp.where(low,f[t],pltpu.roll(f[t^k],16*k,1)) if t&k==0 else jnp.where(low,pltpu.roll(f[t^k],NG-16*k,1),f[t]) for t in range(8)]
        for t in range(8):
            field[(w*8+t)*256:(w*8+t+1)*256,:]=f[t]

    def find(first, last):
        def body(r,carry):
            for h in range(2):
                at=pl.multiple_of(place[2*r+h],2)
                found[pl.ds(pl.multiple_of(4*r+2*h,2),2),:]=field[pl.ds(at,2),:]
            return carry
        lax.fori_loop(first,last,body,0,unroll=32)
        parts=[]
        for h in range(2):
            for o in range(2):
                parts.append(found[pl.ds(4*first+2*h+o,last-first,stride=4),:].astype(BF)*mask[first:last,h*NG:(h+1)*NG])
        return jnp.dot(jnp.concatenate(parts,axis=1),pick[...],preferred_element_type=jnp.float32)

    cols[...]=jnp.broadcast_to(find(ROWS,PTS).astype(BF)[None],(COPIES,COLS,NG))
    send=pltpu.make_async_copy(cols,cols_hbm,sem)
    send.start()
    rows_out[...]=(find(0,ROWS)*weight[...]).astype(BF)
    send.wait()

def point_lists(g_index, slab_index, n_pair,n_grow,n_gcol,grow_at,gcol_at):
    rc=g_index.shape[0]//(n_pair*n_grow*n_gcol)
    cc=slab_index.shape[0]//(n_pair*n_grow*n_gcol)
    row_ids=g_index.reshape(n_pair,n_grow,n_gcol,rc)[:,grow_at,gcol_at]
    row_ids=jnp.pad(row_ids,((0,0),(0,NG-rc)),mode="edge")
    row_ids=jnp.transpose(row_ids.reshape(n_pair,2,64),(0,2,1)).reshape(ROWS,2)
    col_ids=slab_index.reshape(n_gcol,n_pair,n_grow,cc)[gcol_at,:,grow_at]
    col_ids=jnp.transpose(col_ids.reshape(2,COLS),(1,0))
    return jnp.concatenate([row_ids,col_ids],axis=0)

def stage_c(moved, ids, weight):
    q1=ids//(NG*NG); q2=ids//NG%QW; w=ids%PL
    place=((w*8+q2//4)*256+2*q1).reshape(-1)
    lane=jnp.arange(NG,dtype=jnp.int32)//J%4
    mask=((q2%4)[:,:,None]==lane).astype(BF).reshape(PTS,2*NG)
    wl=jnp.tile(weight,4).reshape(1,NG)
    t1,pick=tables_c()
    vm=pl.BlockSpec(memory_space=pltpu.VMEM)
    return pl.pallas_call(kern_c,
        in_specs=[pl.BlockSpec(memory_space=pltpu.SMEM)]+[vm]*5,
        out_specs=[vm,pl.BlockSpec(memory_space=pltpu.HBM)],
        out_shape=[jax.ShapeDtypeStruct((ROWS,NG),BF),jax.ShapeDtypeStruct((COPIES,COLS,NG),BF)],
        scratch_shapes=[pltpu.VMEM((PL*8*256,NG),jnp.float32),pltpu.VMEM((4*PTS,NG),jnp.float32),pltpu.VMEM((COPIES,COLS,NG),BF),pltpu.SemaphoreType.DMA],
        compiler_params=pltpu.CompilerParams(vmem_limit_bytes=40*2**20),
        name="last_transform")(place,moved,t1,pick,mask,wl)

def tables_d():
    q=np.zeros((2,2,2,PAIRS,2,2,2,2,PAIRS))
    for b in range(2):
        for h in range(2):
            for p in range(PAIRS):
                q[b,h,0,p,h,0,b,0,p]=1
                q[b,h,1,p,h,0,b,1,p]=1
                q[b,h,1,p,h,1,b,0,p]=1
                q[b,h,0,p,h,1,b,1,p]=-1
    r=np.zeros((2,2,64,2,2,64))
    for b in range(2):
        for h in range(2):
            for k in range(64):
                r[b,h,k,h,b,k]=1
    return [np.asarray(t,np.float32).astype(ml_dtypes.bfloat16) for t in (q.reshape(256,512),r.reshape(256,256))]

def kern_d(order, rows, cols, turn, halves, out, slab, buf, sems):
    for pp in range(4):
        both=jnp.concatenate([cols[2*pp],cols[2*pp+1]],axis=1)
        v=jnp.dot(both,halves[...],preferred_element_type=jnp.float32)
        v=jnp.concatenate([v[(g*4+pb)*8:(g*4+pb+1)*8] for pb in range(4) for g in range(8)],axis=0).astype(BF)
        for h in range(2):
            slab[h*256:(h+1)*256,pp*NG:(pp+1)*NG]=v[:,h*NG:(h+1)*NG]
    sends=[]
    for c in range(4):
        turned=[]
        for pp in range(4):
            pair=jnp.concatenate([rows[order[c],order[4+2*pp+k]] for k in range(2)],axis=1)
            turned.append(jnp.dot(pair,turn[...],preferred_element_type=jnp.float32).astype(BF))
        lhs=jnp.concatenate([jnp.concatenate([t[:,k*NG:(k+1)*NG] for t in turned],axis=1) for k in range(4)],axis=0)
        z=lax.dot_general(lhs,slab[...],NT,preferred_element_type=jnp.float32)
        for hr in range(2):
            n=64 if hr==0 else 56
            for o in range(2):
                k=hr*2+o
                buf[c,o,64*hr:64*hr+n,:]=z[k*64:k*64+n]
        sends.append(pltpu.make_async_copy(buf.at[c],out.at[:,c],sems.at[c]))
        sends[-1].start()
    for send in sends:
        send.wait()

def stage_d(order, rows, cols):
    vm=pl.BlockSpec(memory_space=pltpu.VMEM)
    return pl.pallas_call(kern_d,
        in_specs=[pl.BlockSpec(memory_space=pltpu.SMEM)]+[vm]*4,out_specs=pl.BlockSpec(memory_space=pltpu.HBM),
        out_shape=jax.ShapeDtypeStruct((2,4,120,512),jnp.float32),
        scratch_shapes=[pltpu.VMEM((512,512),BF),pltpu.VMEM((4,2,120,512),jnp.float32),pltpu.SemaphoreType.DMA((4,))],
        compiler_params=pltpu.CompilerParams(vmem_limit_bytes=32*2**20),
        name="pair_sums")(order,rows,cols,*tables_d()).reshape(2,480,512)

def at(x, k, axis):
    return lax.dynamic_index_in_dim(x, k, axis, False)


def spread_rows(rows, pair_at, gcol_at):
    x_at, y_at = pair_at % 4, pair_at // 4
    both = ("pair", "gcol")
    got = [at(rows, x_at, 1)]
    for d in range(1, 4):
        perm = [(y * 4 + x, y * 4 + (x + d) % 4) for y in range(2) for x in range(4)]
        got.append(lax.ppermute(at(rows, (x_at + d) % 4, 1), "pair", perm))
    got = jnp.stack(got, axis=1)
    own, other = at(got, y_at, 0), at(got, 1 - y_at, 0)

    def swap(block, flip_pair, flip_gcol):
        return lax.ppermute(block, both, [(k, k ^ (flip_pair * 4 + flip_gcol)) for k in range(32)])

    block = jnp.stack([own, swap(other, 4, 0), swap(own, 0, 2), swap(other, 4, 2)]).reshape(2, 8, 64, NG)
    return jnp.concatenate([block, swap(block, 0, 1)])


def on_device(valence, conduction, pair_bands, e_val, e_cond, g_index, slab_index):
    n_pair = lax.axis_size("pair")
    n_grow = lax.axis_size("grow")
    n_gcol = lax.axis_size("gcol")
    pair_at = lax.axis_index("pair")
    grow_at = lax.axis_index("grow")
    gcol_at = lax.axis_index("gcol")
    bands = pair_bands.reshape(-1)
    part = stage_a(valence, conduction, bands)
    moved = lax.all_to_all(part.reshape(32, 8, 4096), ("grow", "gcol"), 0, 0, tiled=True)
    ids = point_lists(g_index, slab_index, n_pair, n_grow, n_gcol, grow_at, gcol_at)
    gaps = jnp.take(e_val, bands) - e_cond[0]
    weight = 2.0 / (gaps * math.sqrt(PAIRS * n_pair))
    rows, cols = stage_c(moved.reshape(256, 4096), ids, weight)
    cols = lax.all_to_all(cols, ("pair", "grow"), 0, 0, tiled=True).reshape(8, 256, NG)
    rows = spread_rows(rows.reshape(2, 4, 64, NG), pair_at, gcol_at)
    c = jnp.arange(4, dtype=jnp.int32)
    blocks = (c % 2 ^ gcol_at % 2) * 2 + (c // 2 ^ gcol_at // 2)
    p = jnp.arange(8, dtype=jnp.int32)
    places = (p // 4 ^ pair_at // 4) * 4 + (pair_at - p) % 4
    return stage_d(jnp.concatenate([blocks, places]).astype(jnp.int32), rows, cols)


def solution(mesh):
    in_specs = (
        P(None, None, ("grow", "gcol"), None),
        P(None, "pair", ("grow", "gcol"), None),
        P("pair", None),
        P(),
        P("pair"),
        P(),
        P(),
    )
    out_specs = P(None, ("pair", "grow"), "gcol")
    return jax.shard_map(
        on_device, mesh=mesh, in_specs=in_specs, out_specs=out_specs, check_vma=False
    )
```

```python
import functools
import math
import numpy as np
import ml_dtypes
import jax
import jax.numpy as jnp
from jax import lax
from jax.sharding import PartitionSpec as P
from jax.experimental import pallas as pl
from jax.experimental.pallas import tpu as pltpu
BF=jnp.bfloat16
VM_A=62
CH=64
NG=128; GR=8; GC=4; PL=4; QW=32; PAIRS=32; J=4
NT=(((1,),(1,)),((),()))
NN=(((1,),(0,)),((),()))

def cs(freq,pos):
    ph=(freq[:,None]*pos[None,:])%NG
    ang=ph.astype(np.float64)*(2*math.pi/NG)
    return np.cos(ang)/math.sqrt(NG), np.sin(ang)/math.sqrt(NG)

def tables():
    ar=np.arange(NG)
    c,w,g=np.meshgrid(np.arange(GC),np.arange(PL),np.arange(GR),indexing="ij")
    q3=((g*GC+c)*PL+w).reshape(-1)
    co,si=cs(q3,ar)
    t3=np.block([[co,si],[-si,co]])
    t2=np.zeros((GC,2,NG,2,QW,J))
    for cc in range(GC):
        co,si=cs(cc*QW+np.arange(QW),ar)
        t2[cc,0,:,0]=co.T[:,:,None]
        t2[cc,1,:,0]=si.T[:,:,None]
        t2[cc,0,:,1]=-si.T[:,:,None]
        t2[cc,1,:,1]=co.T[:,:,None]
    t2=t2.reshape(GC,2*NG,2*J*QW)
    perm=np.zeros((256,256))
    for cc in range(GC):
        for s in range(PL):
            for o in range(2):
                for g_ in range(GR):
                    perm[((g_*GC+cc)*PL+s)*2+o, ((cc*PL+s)*2+o)*GR+g_]=1
    return [np.asarray(t,np.float32).astype(ml_dtypes.bfloat16) for t in (t3,t2,perm)]

def kern_a(Q, steps, bands, val, cnd_hbm, t3_hbm, t2_hbm, perm_hbm, out, vbuf, dens, third, cnd, cond, t3, t2_all, t2, perm, sems, vsems):
    step = pl.program_id(0)
    first = step == 0
    loads = [pltpu.make_async_copy(a, b, sems.at[k]) for k, (a, b) in enumerate(((cnd_hbm, cnd), (t3_hbm, t3), (t2_hbm, t2_all), (perm_hbm, perm)))]

    def band_load(k):
        return pltpu.make_async_copy(val.at[:, bands[k]], vbuf.at[k], vsems.at[k])

    @pl.when(first)
    def _():
        loads[0].start()
        band_load(0).start()
        loads[1].start()
        for k in range(1, Q*J):
            band_load(k).start()
        loads[2].start()
        loads[3].start()
        loads[0].wait()
        cond[...] = cnd[...].astype(jnp.float32)
        loads[1].wait()

    @pl.when(step < steps - 1)
    def _():
        for k in range(Q*J):
            band_load((step+1)*Q*J+k).start()

    for j in range(Q*J):
        k = step*Q*J+j
        band_load(k).wait()
        for r in range(0, NG*PL, CH):
            cr = cond[0, r:r+CH]
            ci = cond[1, r:r+CH]
            vr = vbuf[k, 0, r:r+CH].astype(jnp.float32)
            vi = vbuf[k, 1, r:r+CH].astype(jnp.float32)
            dens[j, 0, r:r+CH] = vr*cr+vi*ci
            dens[j, 1, r:r+CH] = vr*ci-vi*cr
    for j in range(Q*J):
        for sp in range(PL//2):
            rows = []
            for s in (2*sp, 2*sp+1):
                rows.append(jnp.concatenate([dens[j, i, pl.ds(s, NG, stride=PL), :].astype(BF) for i in range(2)], axis=1))
            d = jnp.concatenate(rows, axis=0)
            th = lax.dot_general(t3[...], d, NT, preferred_element_type=jnp.float32)
            third[j, sp] = th.astype(BF)

    @pl.when(first)
    def _():
        loads[2].wait()
        loads[3].wait()
        part = lax.broadcasted_iota(jnp.int32, (2*NG, 2*J*QW), 1) % J
        for c in range(GC):
            for j in range(J):
                t2[c, j*2*NG:(j+1)*2*NG] = jnp.where(part == j, t2_all[c].astype(jnp.float32), 0.0).astype(BF)

    ys=[]
    for c in range(GC):
        lhs=[]
        for q in range(Q):
            for s in range(PL):
                lhs.append(jnp.concatenate([third[q*J+j,s//2,i*NG+c*QW:i*NG+(c+1)*QW,(s%2)*NG:(s%2+1)*NG] for j in range(J) for i in range(2)],axis=1))
        lhs=jnp.concatenate(lhs,axis=0)
        ys.append(jnp.dot(lhs,t2[c],preferred_element_type=jnp.float32))
    for q in range(Q):
        for wp in range(PL//2):
            cols=[]
            for w in (2*wp,2*wp+1):
                pieces=[ys[c][(q*PL+s)*QW+w*GR:(q*PL+s)*QW+(w+1)*GR,o*NG:(o+1)*NG] for c in range(GC) for s in range(PL) for o in range(2)]
                cols.append(jnp.concatenate(pieces,axis=0).astype(BF))
            y=jnp.concatenate(cols,axis=1)
            out[:,(q*2+wp)*256:(q*2+wp+1)*256]=jnp.dot(perm[...],y,preferred_element_type=jnp.float32).astype(BF)


def stage_a(valence, cond, bands, Q=4):
    nval=valence.shape[1]
    v=jnp.transpose(valence.reshape(2,nval,PL,NG,NG),(0,1,3,2,4)).reshape(2,nval,NG*PL,NG)
    cf=jnp.transpose(cond.reshape(2,PL,NG,NG),(0,2,1,3)).reshape(2,NG*PL,NG)
    t3,t2,perm=tables()
    steps=bands.shape[0]//(Q*J)
    return pl.pallas_call(functools.partial(kern_a,Q,steps),
        grid_spec=pltpu.PrefetchScalarGridSpec(num_scalar_prefetch=1,grid=(steps,),
            in_specs=[pl.BlockSpec(memory_space=pltpu.HBM)]*5,
            out_specs=pl.BlockSpec((256,512*Q),lambda q,b:(0,q)),
            scratch_shapes=[pltpu.VMEM((PAIRS,2,NG*PL,NG),BF),pltpu.VMEM((Q*J,2,NG*PL,NG),jnp.float32),pltpu.VMEM((Q*J,PL//2,256,256),BF),pltpu.VMEM((2,NG*PL,NG),BF),pltpu.VMEM((2,NG*PL,NG),jnp.float32),pltpu.VMEM((256,256),BF),
                pltpu.VMEM((GC,256,256),BF),pltpu.VMEM((GC,1024,256),BF),pltpu.VMEM((256,256),BF),
                pltpu.SemaphoreType.DMA((4,)),pltpu.SemaphoreType.DMA((PAIRS,))]),
        out_shape=jax.ShapeDtypeStruct((256,bands.shape[0]//J*512),BF),
        compiler_params=pltpu.CompilerParams(vmem_limit_bytes=VM_A*2**20),
        name="partial_transform")(bands,v,cf,t3,t2,perm)

ROWS=GR*64; COLS=32; COPIES=64; PTS=ROWS+COLS

def tables_c():
    ar=np.arange(NG)
    co,si=cs(ar,ar)
    t1=np.zeros((NG,2,NG,2))
    t1[:,0,:,0]=co; t1[:,0,:,1]=si; t1[:,1,:,0]=-si; t1[:,1,:,1]=co
    t1=t1.reshape(256,256)
    pick=np.zeros((2,2,8,4,J,2,2,8,J))
    for h in range(2):
        for o in range(2):
            for q in range(8):
                for j in range(J):
                    pick[h,o,q,:,j,h,o,q,j]=1
    pick=pick.reshape(512,128)
    return [np.asarray(t,np.float32).astype(ml_dtypes.bfloat16) for t in (t1,pick)]

def kern_c(place, x, t1, pick, mask, weight, rows_out, cols_hbm, field, found, cols, sem):
    group=lax.broadcasted_iota(jnp.int32,(256,NG),1)//16
    for w in range(PL):
        xw=jnp.concatenate([x[:,(q*PL+w)*NG:(q*PL+w+1)*NG] for q in range(8)],axis=1)
        f=jnp.dot(t1[...],xw,preferred_element_type=jnp.float32).astype(BF).astype(jnp.float32)
        f=[f[:,t*NG:(t+1)*NG] for t in range(8)]
        for k in (1,2,4):
            low=group//k%2==0
            f=[jnp.where(low,f[t],pltpu.roll(f[t^k],16*k,1)) if t&k==0 else jnp.where(low,pltpu.roll(f[t^k],NG-16*k,1),f[t]) for t in range(8)]
        for t in range(8):
            field[(w*8+t)*256:(w*8+t+1)*256,:]=f[t]

    def find(first, last):
        def body(r,carry):
            for h in range(2):
                at=pl.multiple_of(place[2*r+h],2)
                found[pl.ds(pl.multiple_of(4*r+2*h,2),2),:]=field[pl.ds(at,2),:]
            return carry
        lax.fori_loop(first,last,body,0,unroll=32)
        parts=[]
        for h in range(2):
            for o in range(2):
                parts.append(found[pl.ds(4*first+2*h+o,last-first,stride=4),:].astype(BF)*mask[first:last,h*NG:(h+1)*NG])
        return jnp.dot(jnp.concatenate(parts,axis=1),pick[...],preferred_element_type=jnp.float32)

    cols[...]=jnp.broadcast_to(find(ROWS,PTS).astype(BF)[None],(COPIES,COLS,NG))
    send=pltpu.make_async_copy(cols,cols_hbm,sem)
    send.start()
    rows_out[...]=(find(0,ROWS)*weight[...]).astype(BF)
    send.wait()

def point_lists(g_index, slab_index, n_pair,n_grow,n_gcol,grow_at,gcol_at):
    rc=g_index.shape[0]//(n_pair*n_grow*n_gcol)
    cc=slab_index.shape[0]//(n_pair*n_grow*n_gcol)
    row_ids=g_index.reshape(n_pair,n_grow,n_gcol,rc)[:,grow_at,gcol_at]
    row_ids=jnp.pad(row_ids,((0,0),(0,NG-rc)),mode="edge")
    row_ids=jnp.transpose(row_ids.reshape(n_pair,2,64),(0,2,1)).reshape(ROWS,2)
    col_ids=slab_index.reshape(n_gcol,n_pair,n_grow,cc)[gcol_at,:,grow_at]
    col_ids=jnp.transpose(col_ids.reshape(2,COLS),(1,0))
    return jnp.concatenate([row_ids,col_ids],axis=0)

def stage_c(moved, ids, weight):
    q1=ids//(NG*NG); q2=ids//NG%QW; w=ids%PL
    place=((w*8+q2//4)*256+2*q1).reshape(-1)
    lane=jnp.arange(NG,dtype=jnp.int32)//J%4
    mask=((q2%4)[:,:,None]==lane).astype(BF).reshape(PTS,2*NG)
    wl=jnp.tile(weight,4).reshape(1,NG)
    t1,pick=tables_c()
    vm=pl.BlockSpec(memory_space=pltpu.VMEM)
    return pl.pallas_call(kern_c,
        in_specs=[pl.BlockSpec(memory_space=pltpu.SMEM)]+[vm]*5,
        out_specs=[vm,pl.BlockSpec(memory_space=pltpu.HBM)],
        out_shape=[jax.ShapeDtypeStruct((ROWS,NG),BF),jax.ShapeDtypeStruct((COPIES,COLS,NG),BF)],
        scratch_shapes=[pltpu.VMEM((PL*8*256,NG),jnp.float32),pltpu.VMEM((4*PTS,NG),jnp.float32),pltpu.VMEM((COPIES,COLS,NG),BF),pltpu.SemaphoreType.DMA],
        compiler_params=pltpu.CompilerParams(vmem_limit_bytes=40*2**20),
        name="last_transform")(place,moved,t1,pick,mask,wl)

def tables_d():
    q=np.zeros((2,2,2,PAIRS,2,2,2,2,PAIRS))
    for b in range(2):
        for h in range(2):
            for p in range(PAIRS):
                q[b,h,0,p,h,0,b,0,p]=1
                q[b,h,1,p,h,0,b,1,p]=1
                q[b,h,1,p,h,1,b,0,p]=1
                q[b,h,0,p,h,1,b,1,p]=-1
    r=np.zeros((2,2,64,2,2,64))
    for b in range(2):
        for h in range(2):
            for k in range(64):
                r[b,h,k,h,b,k]=1
    return [np.asarray(t,np.float32).astype(ml_dtypes.bfloat16) for t in (q.reshape(256,512),r.reshape(256,256))]

def kern_d(order, rows, cols, turn, halves, out, slab, buf, sems):
    for pp in range(4):
        both=jnp.concatenate([jnp.concatenate([cols[g*8+2*pp+k] for g in range(8)],axis=0) for k in range(2)],axis=1)
        v=jnp.dot(both,halves[...],preferred_element_type=jnp.float32)
        v=jnp.concatenate([v[(g*4+pb)*8:(g*4+pb+1)*8] for pb in range(4) for g in range(8)],axis=0).astype(BF)
        for h in range(2):
            slab[h*256:(h+1)*256,pp*NG:(pp+1)*NG]=v[:,h*NG:(h+1)*NG]
    sends=[]
    for c in range(4):
        turned=[]
        for pp in range(4):
            pair=jnp.concatenate([rows[order[c],order[4+2*pp+k]] for k in range(2)],axis=1)
            turned.append(jnp.dot(pair,turn[...],preferred_element_type=jnp.float32).astype(BF))
        lhs=jnp.concatenate([jnp.concatenate([t[:,k*NG:(k+1)*NG] for t in turned],axis=1) for k in range(4)],axis=0)
        z=lax.dot_general(lhs,slab[...],NT,preferred_element_type=jnp.float32)
        for hr in range(2):
            n=64 if hr==0 else 56
            for o in range(2):
                k=hr*2+o
                buf[c,o,64*hr:64*hr+n,:]=z[k*64:k*64+n]
        sends.append(pltpu.make_async_copy(buf.at[c],out.at[:,c],sems.at[c]))
        sends[-1].start()
    for send in sends:
        send.wait()

def stage_d(order, rows, cols):
    vm=pl.BlockSpec(memory_space=pltpu.VMEM)
    return pl.pallas_call(kern_d,
        in_specs=[pl.BlockSpec(memory_space=pltpu.SMEM)]+[vm]*4,out_specs=pl.BlockSpec(memory_space=pltpu.HBM),
        out_shape=jax.ShapeDtypeStruct((2,4,120,512),jnp.float32),
        scratch_shapes=[pltpu.VMEM((512,512),BF),pltpu.VMEM((4,2,120,512),jnp.float32),pltpu.SemaphoreType.DMA((4,))],
        compiler_params=pltpu.CompilerParams(vmem_limit_bytes=32*2**20),
        name="pair_sums")(order,rows,cols,*tables_d()).reshape(2,480,512)

def at(x, k, axis):
    return lax.dynamic_index_in_dim(x, k, axis, False)


def spread_rows(rows, pair_at, gcol_at):
    x_at, y_at = pair_at % 4, pair_at // 4
    both = ("pair", "gcol")
    got = [at(rows, x_at, 1)]
    for d in range(1, 4):
        perm = [(y * 4 + x, y * 4 + (x + d) % 4) for y in range(2) for x in range(4)]
        got.append(lax.ppermute(at(rows, (x_at + d) % 4, 1), "pair", perm))
    got = jnp.stack(got, axis=1)
    own, other = at(got, y_at, 0), at(got, 1 - y_at, 0)

    def swap(block, flip_pair, flip_gcol):
        return lax.ppermute(block, both, [(k, k ^ (flip_pair * 4 + flip_gcol)) for k in range(32)])

    block = jnp.stack([own, swap(other, 4, 0), swap(own, 0, 2), swap(other, 4, 2)]).reshape(2, 8, 64, NG)
    return jnp.concatenate([block, swap(block, 0, 1)])


def on_device(valence, conduction, pair_bands, e_val, e_cond, g_index, slab_index):
    n_pair = lax.axis_size("pair")
    n_grow = lax.axis_size("grow")
    n_gcol = lax.axis_size("gcol")
    pair_at = lax.axis_index("pair")
    grow_at = lax.axis_index("grow")
    gcol_at = lax.axis_index("gcol")
    bands = pair_bands.reshape(-1)
    part = stage_a(valence, conduction, bands)
    moved = lax.all_to_all(part.reshape(32, 8, 4096), ("grow", "gcol"), 0, 0, tiled=True)
    ids = point_lists(g_index, slab_index, n_pair, n_grow, n_gcol, grow_at, gcol_at)
    gaps = jnp.take(e_val, bands) - e_cond[0]
    weight = 2.0 / (gaps * math.sqrt(PAIRS * n_pair))
    rows, cols = stage_c(moved.reshape(256, 4096), ids, weight)
    cols = lax.all_to_all(cols, ("grow", "pair"), 0, 0, tiled=True)
    rows = spread_rows(rows.reshape(2, 4, 64, NG), pair_at, gcol_at)
    c = jnp.arange(4, dtype=jnp.int32)
    blocks = (c % 2 ^ gcol_at % 2) * 2 + (c // 2 ^ gcol_at // 2)
    p = jnp.arange(8, dtype=jnp.int32)
    places = (p // 4 ^ pair_at // 4) * 4 + (pair_at - p) % 4
    return stage_d(jnp.concatenate([blocks, places]).astype(jnp.int32), rows, cols)


def solution(mesh):
    in_specs = (
        P(None, None, ("grow", "gcol"), None),
        P(None, "pair", ("grow", "gcol"), None),
        P("pair", None),
        P(),
        P("pair"),
        P(),
        P(),
    )
    out_specs = P(None, ("pair", "grow"), "gcol")
    return jax.shard_map(
        on_device, mesh=mesh, in_specs=in_specs, out_specs=out_specs, check_vma=False
    )
```

```python
import functools
import math
import numpy as np
import ml_dtypes
import jax
import jax.numpy as jnp
from jax import lax
from jax.sharding import PartitionSpec as P
from jax.experimental import pallas as pl
from jax.experimental.pallas import tpu as pltpu
BF=jnp.bfloat16
VM_A=62
CH=64
NG=128; GR=8; GC=4; PL=4; QW=32; PAIRS=32; J=4
NT=(((1,),(1,)),((),()))
NN=(((1,),(0,)),((),()))

def cs(freq,pos):
    ph=(freq[:,None]*pos[None,:])%NG
    ang=ph.astype(np.float64)*(2*math.pi/NG)
    return np.cos(ang)/math.sqrt(NG), np.sin(ang)/math.sqrt(NG)

def tables():
    ar=np.arange(NG)
    c,w,g=np.meshgrid(np.arange(GC),np.arange(PL),np.arange(GR),indexing="ij")
    q3=((g*GC+c)*PL+w).reshape(-1)
    co,si=cs(q3,ar)
    t3=np.block([[co,si],[-si,co]])
    t2=np.zeros((GC,2,NG,2,QW,J))
    for cc in range(GC):
        co,si=cs(cc*QW+np.arange(QW),ar)
        t2[cc,0,:,0]=co.T[:,:,None]
        t2[cc,1,:,0]=si.T[:,:,None]
        t2[cc,0,:,1]=-si.T[:,:,None]
        t2[cc,1,:,1]=co.T[:,:,None]
    t2=t2.reshape(GC,2*NG,2*J*QW)
    perm=np.zeros((256,256))
    for cc in range(GC):
        for s in range(PL):
            for o in range(2):
                for g_ in range(GR):
                    perm[((g_*GC+cc)*PL+s)*2+o, ((cc*PL+s)*2+o)*GR+g_]=1
    return [np.asarray(t,np.float32).astype(ml_dtypes.bfloat16) for t in (t3,t2,perm)]

def kern_a(Q, steps, bands, val, cnd_hbm, t3_hbm, t2_hbm, perm_hbm, out, vbuf, dens, third, cnd, cond, t3, t2_all, t2, perm, sems, vsems):
    step = pl.program_id(0)
    first = step == 0
    loads = [pltpu.make_async_copy(a, b, sems.at[k]) for k, (a, b) in enumerate(((cnd_hbm, cnd), (t3_hbm, t3), (t2_hbm, t2_all), (perm_hbm, perm)))]

    def band_load(k):
        return pltpu.make_async_copy(val.at[:, bands[k]], vbuf.at[k], vsems.at[k])

    @pl.when(first)
    def _():
        loads[0].start()
        band_load(0).start()
        loads[1].start()
        for k in range(1, Q*J):
            band_load(k).start()
        loads[2].start()
        loads[3].start()
        loads[0].wait()
        cond[...] = cnd[...].astype(jnp.float32)
        loads[1].wait()

    @pl.when(step < steps - 1)
    def _():
        for k in range(Q*J):
            band_load((step+1)*Q*J+k).start()

    for j in range(Q*J):
        k = step*Q*J+j
        band_load(k).wait()
        for r in range(0, NG*PL, CH):
            cr = cond[0, r:r+CH]
            ci = cond[1, r:r+CH]
            vr = vbuf[k, 0, r:r+CH].astype(jnp.float32)
            vi = vbuf[k, 1, r:r+CH].astype(jnp.float32)
            dens[j, 0, r:r+CH] = vr*cr+vi*ci
            dens[j, 1, r:r+CH] = vr*ci-vi*cr
    for j in range(Q*J):
        for sp in range(PL//2):
            rows = []
            for s in (2*sp, 2*sp+1):
                rows.append(jnp.concatenate([dens[j, i, pl.ds(s, NG, stride=PL), :].astype(BF) for i in range(2)], axis=1))
            d = jnp.concatenate(rows, axis=0)
            th = lax.dot_general(t3[...], d, NT, preferred_element_type=jnp.float32)
            third[j, sp] = th.astype(BF)

    @pl.when(first)
    def _():
        loads[2].wait()
        loads[3].wait()
        part = lax.broadcasted_iota(jnp.int32, (2*NG, 2*J*QW), 1) % J
        for c in range(GC):
            for j in range(J):
                t2[c, j*2*NG:(j+1)*2*NG] = jnp.where(part == j, t2_all[c].astype(jnp.float32), 0.0).astype(BF)

    ys=[]
    for c in range(GC):
        lhs=[]
        for q in range(Q):
            for s in range(PL):
                lhs.append(jnp.concatenate([third[q*J+j,s//2,i*NG+c*QW:i*NG+(c+1)*QW,(s%2)*NG:(s%2+1)*NG] for j in range(J) for i in range(2)],axis=1))
        lhs=jnp.concatenate(lhs,axis=0)
        ys.append(jnp.dot(lhs,t2[c],preferred_element_type=jnp.float32))
    for q in range(Q):
        for wp in range(PL//2):
            cols=[]
            for w in (2*wp,2*wp+1):
                pieces=[ys[c][(q*PL+s)*QW+w*GR:(q*PL+s)*QW+(w+1)*GR,o*NG:(o+1)*NG] for c in range(GC) for s in range(PL) for o in range(2)]
                cols.append(jnp.concatenate(pieces,axis=0).astype(BF))
            y=jnp.concatenate(cols,axis=1)
            out[:,(q*2+wp)*256:(q*2+wp+1)*256]=jnp.dot(perm[...],y,preferred_element_type=jnp.float32).astype(BF)


def stage_a(valence, cond, bands, Q=4):
    nval=valence.shape[1]
    v=jnp.transpose(valence.reshape(2,nval,PL,NG,NG),(0,1,3,2,4)).reshape(2,nval,NG*PL,NG)
    cf=jnp.transpose(cond.reshape(2,PL,NG,NG),(0,2,1,3)).reshape(2,NG*PL,NG)
    t3,t2,perm=tables()
    steps=bands.shape[0]//(Q*J)
    return pl.pallas_call(functools.partial(kern_a,Q,steps),
        grid_spec=pltpu.PrefetchScalarGridSpec(num_scalar_prefetch=1,grid=(steps,),
            in_specs=[pl.BlockSpec(memory_space=pltpu.HBM)]*5,
            out_specs=pl.BlockSpec((256,512*Q),lambda q,b:(0,q)),
            scratch_shapes=[pltpu.VMEM((PAIRS,2,NG*PL,NG),BF),pltpu.VMEM((Q*J,2,NG*PL,NG),jnp.float32),pltpu.VMEM((Q*J,PL//2,256,256),BF),pltpu.VMEM((2,NG*PL,NG),BF),pltpu.VMEM((2,NG*PL,NG),jnp.float32),pltpu.VMEM((256,256),BF),
                pltpu.VMEM((GC,256,256),BF),pltpu.VMEM((GC,1024,256),BF),pltpu.VMEM((256,256),BF),
                pltpu.SemaphoreType.DMA((4,)),pltpu.SemaphoreType.DMA((PAIRS,))]),
        out_shape=jax.ShapeDtypeStruct((256,bands.shape[0]//J*512),BF),
        compiler_params=pltpu.CompilerParams(vmem_limit_bytes=VM_A*2**20),
        name="partial_transform")(bands,v,cf,t3,t2,perm)

ROWS=GR*64; COLS=32; COPIES=64; PTS=ROWS+COLS

def tables_c():
    ar=np.arange(NG)
    co,si=cs(ar,ar)
    t1=np.zeros((NG,2,NG,2))
    t1[:,0,:,0]=co; t1[:,0,:,1]=si; t1[:,1,:,0]=-si; t1[:,1,:,1]=co
    t1=t1.reshape(256,256)
    pick=np.zeros((2,2,8,4,J,2,2,8,J))
    for h in range(2):
        for o in range(2):
            for q in range(8):
                for j in range(J):
                    pick[h,o,q,:,j,h,o,q,j]=1
    pick=pick.reshape(512,128)
    return [np.asarray(t,np.float32).astype(ml_dtypes.bfloat16) for t in (t1,pick)]

def kern_c(place, x, t1, pick, mask, weight, rows_out, cols_hbm, field, found, cols, sem):
    group=lax.broadcasted_iota(jnp.int32,(256,NG),1)//16
    for w in range(PL):
        xw=jnp.concatenate([x[:,(q*PL+w)*NG:(q*PL+w+1)*NG] for q in range(8)],axis=1)
        f=jnp.dot(t1[...],xw,preferred_element_type=jnp.float32).astype(BF)
        f=[f[:,t*NG:(t+1)*NG] for t in range(8)]
        for k in (1,2,4):
            low=group//k%2==0
            f=[jnp.where(low,f[t],pltpu.roll(f[t^k],16*k,1)) if t&k==0 else jnp.where(low,pltpu.roll(f[t^k],NG-16*k,1),f[t]) for t in range(8)]
        for t in range(8):
            field[(w*8+t)*256:(w*8+t+1)*256,:]=f[t].astype(jnp.float32)

    def find(first, last):
        def body(r,carry):
            for h in range(2):
                at=pl.multiple_of(place[2*r+h],2)
                found[pl.ds(pl.multiple_of(4*r+2*h,2),2),:]=field[pl.ds(at,2),:]
            return carry
        lax.fori_loop(first,last,body,0,unroll=32)
        parts=[]
        for h in range(2):
            for o in range(2):
                parts.append(found[pl.ds(4*first+2*h+o,last-first,stride=4),:].astype(BF)*mask[first:last,h*NG:(h+1)*NG])
        return jnp.dot(jnp.concatenate(parts,axis=1),pick[...],preferred_element_type=jnp.float32)

    cols[...]=jnp.broadcast_to(find(ROWS,PTS).astype(BF)[None],(COPIES,COLS,NG))
    send=pltpu.make_async_copy(cols,cols_hbm,sem)
    send.start()
    rows_out[...]=(find(0,ROWS)*weight[...]).astype(BF)
    send.wait()

def point_lists(g_index, slab_index, n_pair,n_grow,n_gcol,grow_at,gcol_at):
    rc=g_index.shape[0]//(n_pair*n_grow*n_gcol)
    cc=slab_index.shape[0]//(n_pair*n_grow*n_gcol)
    row_ids=g_index.reshape(n_pair,n_grow,n_gcol,rc)[:,grow_at,gcol_at]
    row_ids=jnp.pad(row_ids,((0,0),(0,NG-rc)),mode="edge")
    row_ids=jnp.transpose(row_ids.reshape(n_pair,2,64),(0,2,1)).reshape(ROWS,2)
    col_ids=slab_index.reshape(n_gcol,n_pair,n_grow,cc)[gcol_at,:,grow_at]
    col_ids=jnp.transpose(col_ids.reshape(2,COLS),(1,0))
    return jnp.concatenate([row_ids,col_ids],axis=0)

def stage_c(moved, ids, weight):
    q1=ids//(NG*NG); q2=ids//NG%QW; w=ids%PL
    place=((w*8+q2//4)*256+2*q1).reshape(-1)
    lane=jnp.arange(NG,dtype=jnp.int32)//J%4
    mask=((q2%4)[:,:,None]==lane).astype(BF).reshape(PTS,2*NG)
    wl=jnp.tile(weight,4).reshape(1,NG)
    t1,pick=tables_c()
    vm=pl.BlockSpec(memory_space=pltpu.VMEM)
    return pl.pallas_call(kern_c,
        in_specs=[pl.BlockSpec(memory_space=pltpu.SMEM)]+[vm]*5,
        out_specs=[vm,pl.BlockSpec(memory_space=pltpu.HBM)],
        out_shape=[jax.ShapeDtypeStruct((ROWS,NG),BF),jax.ShapeDtypeStruct((COPIES,COLS,NG),BF)],
        scratch_shapes=[pltpu.VMEM((PL*8*256,NG),jnp.float32),pltpu.VMEM((4*PTS,NG),jnp.float32),pltpu.VMEM((COPIES,COLS,NG),BF),pltpu.SemaphoreType.DMA],
        compiler_params=pltpu.CompilerParams(vmem_limit_bytes=40*2**20),
        name="last_transform")(place,moved,t1,pick,mask,wl)

def tables_d():
    q=np.zeros((2,2,2,PAIRS,2,2,2,2,PAIRS))
    for b in range(2):
        for h in range(2):
            for p in range(PAIRS):
                q[b,h,0,p,h,0,b,0,p]=1
                q[b,h,1,p,h,0,b,1,p]=1
                q[b,h,1,p,h,1,b,0,p]=1
                q[b,h,0,p,h,1,b,1,p]=-1
    r=np.zeros((2,2,64,2,2,64))
    for b in range(2):
        for h in range(2):
            for k in range(64):
                r[b,h,k,h,b,k]=1
    return [np.asarray(t,np.float32).astype(ml_dtypes.bfloat16) for t in (q.reshape(256,512),r.reshape(256,256))]

def kern_d(order, rows, cols, turn, halves, out, slab, buf, sems):
    for pp in range(4):
        both=jnp.concatenate([jnp.concatenate([cols[g*8+2*pp+k] for g in range(8)],axis=0) for k in range(2)],axis=1)
        v=jnp.dot(both,halves[...],preferred_element_type=jnp.float32)
        v=jnp.concatenate([v[(g*4+pb)*8:(g*4+pb+1)*8] for pb in range(4) for g in range(8)],axis=0).astype(BF)
        for h in range(2):
            slab[h*256:(h+1)*256,pp*NG:(pp+1)*NG]=v[:,h*NG:(h+1)*NG]
    sends=[]
    for c in range(4):
        turned=[]
        for pp in range(4):
            pair=jnp.concatenate([rows[order[c],order[4+2*pp+k]] for k in range(2)],axis=1)
            turned.append(jnp.dot(pair,turn[...],preferred_element_type=jnp.float32).astype(BF))
        lhs=jnp.concatenate([jnp.concatenate([t[:,k*NG:(k+1)*NG] for t in turned],axis=1) for k in range(4)],axis=0)
        z=lax.dot_general(lhs,slab[...],NT,preferred_element_type=jnp.float32)
        for hr in range(2):
            n=64 if hr==0 else 56
            for o in range(2):
                k=hr*2+o
                buf[c,o,64*hr:64*hr+n,:]=z[k*64:k*64+n]
        sends.append(pltpu.make_async_copy(buf.at[c],out.at[:,c],sems.at[c]))
        sends[-1].start()
    for send in sends:
        send.wait()

def stage_d(order, rows, cols):
    vm=pl.BlockSpec(memory_space=pltpu.VMEM)
    return pl.pallas_call(kern_d,
        in_specs=[pl.BlockSpec(memory_space=pltpu.SMEM)]+[vm]*4,out_specs=pl.BlockSpec(memory_space=pltpu.HBM),
        out_shape=jax.ShapeDtypeStruct((2,4,120,512),jnp.float32),
        scratch_shapes=[pltpu.VMEM((512,512),BF),pltpu.VMEM((4,2,120,512),jnp.float32),pltpu.SemaphoreType.DMA((4,))],
        compiler_params=pltpu.CompilerParams(vmem_limit_bytes=32*2**20),
        name="pair_sums")(order,rows,cols,*tables_d()).reshape(2,480,512)

def at(x, k, axis):
    return lax.dynamic_index_in_dim(x, k, axis, False)


def spread_rows(rows, pair_at, gcol_at):
    x_at, y_at = pair_at % 4, pair_at // 4
    both = ("pair", "gcol")
    got = [at(rows, x_at, 1)]
    for d in (1, 3, 2):
        perm = [(y * 4 + x, y * 4 + (x + d) % 4) for y in range(2) for x in range(4)]
        got.append(lax.ppermute(at(rows, (x_at + d) % 4, 1), "pair", perm))
    got = jnp.stack([got[0], got[1], got[3], got[2]], axis=1)
    own, other = at(got, y_at, 0), at(got, 1 - y_at, 0)

    def swap(block, flip_pair, flip_gcol):
        return lax.ppermute(block, both, [(k, k ^ (flip_pair * 4 + flip_gcol)) for k in range(32)])

    block = jnp.stack([own, swap(other, 4, 0), swap(own, 0, 2), swap(other, 4, 2)]).reshape(2, 8, 64, NG)
    return jnp.concatenate([block, swap(block, 0, 1)])


def on_device(valence, conduction, pair_bands, e_val, e_cond, g_index, slab_index):
    n_pair = lax.axis_size("pair")
    n_grow = lax.axis_size("grow")
    n_gcol = lax.axis_size("gcol")
    pair_at = lax.axis_index("pair")
    grow_at = lax.axis_index("grow")
    gcol_at = lax.axis_index("gcol")
    bands = pair_bands.reshape(-1)
    part = stage_a(valence, conduction, bands)
    moved = lax.all_to_all(part.reshape(32, 8, 4096), ("grow", "gcol"), 0, 0, tiled=True)
    ids = point_lists(g_index, slab_index, n_pair, n_grow, n_gcol, grow_at, gcol_at)
    gaps = jnp.take(e_val, bands) - e_cond[0]
    weight = 2.0 / (gaps * math.sqrt(PAIRS * n_pair))
    rows, cols = stage_c(moved.reshape(256, 4096), ids, weight)
    cols = lax.all_to_all(cols, ("grow", "pair"), 0, 0, tiled=True)
    rows = spread_rows(rows.reshape(2, 4, 64, NG), pair_at, gcol_at)
    c = jnp.arange(4, dtype=jnp.int32)
    blocks = (c % 2 ^ gcol_at % 2) * 2 + (c // 2 ^ gcol_at // 2)
    p = jnp.arange(8, dtype=jnp.int32)
    places = (p // 4 ^ pair_at // 4) * 4 + (pair_at - p) % 4
    return stage_d(jnp.concatenate([blocks, places]).astype(jnp.int32), rows, cols)


def solution(mesh):
    in_specs = (
        P(None, None, ("grow", "gcol"), None),
        P(None, "pair", ("grow", "gcol"), None),
        P("pair", None),
        P(),
        P("pair"),
        P(),
        P(),
    )
    out_specs = P(None, ("pair", "grow"), "gcol")
    return jax.shard_map(
        on_device, mesh=mesh, in_specs=in_specs, out_specs=out_specs, check_vma=False
    )
```
